256 devices in a mesh: seq: 32 (over z, x_lo, core), head: 8 (over x_hi, y).
Axes of the slice: x: 4 (x_hi: 2, x_lo: 2; x = x_hi * 2 + x_lo), y: 4, z: 8, core: 2. Of those that a mesh axis runs over, the one named last changes fastest.
Arguments:
- queries: bfloat16 [6144, 5120], P('seq', 'head'), may hold values from -8 to 8
- cur_keys: bfloat16 [6144, 5120], P('seq', 'head'), may hold values from -8 to 8
- cur_values: bfloat16 [6144, 5120], P('seq', 'head'), may hold values from -6 to 6
- hist_keys: bfloat16 [14336, 5120], P('seq', 'head'), may hold values from -8 to 8
- hist_values: bfloat16 [14336, 5120], P('seq', 'head'), may hold values from -6 to 6
- piece_readers: int32 [448, 2], P('seq'), may hold values from 0 to 31, as said below
- out_weight: bfloat16 [5120, 5120], P('head'), may hold values from -0.3125 to 0.3125
Outputs:
- attn_out: bfloat16 [6144, 5120], P('seq', 'head')
The draws below stay inside these ranges and needn't reach their ends.
Inputs may be any that keep to these rules, and one draw needn't show every extreme that they name: `piece_readers`: row j names 2 different reader blocks (indices of seq); piece j is held by index j // 14 of seq. One holder sends at most 2 pieces to one reader block: each holder sends to exactly 14 reader blocks, 2 pieces to each, and in every draw one reader block receives 2 pieces from every holder.
All inputs are finite; a program needn't handle non-finite values.
Results may differ from the reference program's by a relative error of at most 0.018.
Values may be sent and summed in bfloat16 or wider, within the bound.
No kernel may reach another device: no remote copies, remote signals or barrier semaphores. Data moves between devices by JAX's collectives and lax.ppermute only.
A program may use at most 192 MiB of HBM per device.

```python
import math
import jax
import jax.numpy as jnp
from jax import lax

HEADS = 40
HDIM = 128
D = 5120
TOK_DEV = 192
TOKENS = 6144
PIECE = 32
HP_DEV = 14
TOP = 2
CAP = 2
READERS = 32
HPIECES = 448
HISTORY = 14336


def draw_queries(key, part):
    key = jax.random.fold_in(key, 11)
    own_rows = 1.6 * jax.random.normal(key, (TOKENS, D), jnp.float32)
    return jnp.clip(own_rows, -8.0, 8.0).astype(jnp.bfloat16)


def draw_cur_keys(key, part):
    key = jax.random.fold_in(key, 12)
    own_rows = 1.6 * jax.random.normal(key, (TOKENS, D), jnp.float32)
    return jnp.clip(own_rows, -8.0, 8.0).astype(jnp.bfloat16)


def draw_piece_readers(key, part):
    key = jax.random.fold_in(key, 21)
    hot_key, order_key, rank_key = jax.random.split(key, 3)
    hot_reader = jax.random.randint(hot_key, (), 0, READERS)
    reader_ids = jnp.arange(READERS, dtype=jnp.int32)
    order_noise = jax.random.randint(order_key, (READERS, READERS), 0, 1 << 20)
    order_score = order_noise * READERS + reader_ids[None, :]
    order_score = jnp.where(reader_ids[None, :] == hot_reader, -1, order_score)
    reader_order = jnp.argsort(order_score, axis=1).astype(jnp.int32)
    rank_noise = jax.random.randint(rank_key, (READERS, TOP, HP_DEV), 0, 1 << 20)
    rank_score = rank_noise * HP_DEV + jnp.arange(HP_DEV, dtype=jnp.int32)[None, None, :]
    piece_rank = jnp.argsort(rank_score, axis=2).astype(jnp.int32)
    top_ids = jnp.arange(TOP, dtype=jnp.int32)
    slot_ids = top_ids[None, :, None] * (HP_DEV // CAP) + piece_rank // CAP
    spread_order = jnp.broadcast_to(reader_order[:, None, :], (READERS, TOP, READERS))
    chosen = jnp.take_along_axis(spread_order, slot_ids, axis=2)
    return jnp.transpose(chosen, (0, 2, 1)).reshape(HPIECES, TOP).astype(jnp.int32)


def block_levels(own_key, extent, cuts, least, high):
    level = 1.0
    for position, shards_of in cuts:
        heights = jax.random.uniform(jax.random.fold_in(jax.random.fold_in(own_key, 6), position), (shards_of,), jnp.float32, least / len(cuts), high / len(cuts))
        level = level * jnp.repeat(jnp.exp(heights), extent[position] // shards_of).reshape((-1,) + (1,) * (len(extent) - 1 - position))
    return level


def gaussian(rng, extent, deviation, bound, pieces=(), held_as=jnp.bfloat16):
    gain = block_levels(rng, extent, pieces, -0.22, 0.18) if pieces else 1.0
    drawn = jax.random.normal(rng, extent, jnp.float32) * deviation * gain
    return jnp.minimum(jnp.maximum(drawn, -bound), bound).astype(held_as)


def setup_inputs(seed: int = 0) -> dict:
    splits = jax.random.split(jax.random.key(seed), 8)
    return {
        "queries": draw_queries(jax.random.fold_in(splits[7], 71), 0),
        "cur_keys": draw_cur_keys(jax.random.fold_in(splits[7], 71), 0),
        "cur_values": gaussian(splits[2], (TOKENS, D), 1.0, 6.0, ((0, 32), (1, 8))),
        "hist_keys": gaussian(splits[3], (HISTORY, D), 1.6, 8.0, ((0, 32), (1, 8))),
        "hist_values": gaussian(splits[4], (HISTORY, D), 1.0, 6.0, ((0, 32), (1, 8))),
        "piece_readers": draw_piece_readers(jax.random.fold_in(splits[7], 71), 0),
        "out_weight": gaussian(splits[6], (D, D), (D // 16) ** -0.5, 0.3125, ((0, 8),)),
    }


def reference(queries, cur_keys, cur_values, hist_keys, hist_values, piece_readers, out_weight):
    scale = 1.0 / math.sqrt(HDIM)
    query_blocks = queries.reshape(READERS, TOK_DEV, HEADS, HDIM)
    key_cur = cur_keys.astype(jnp.float32).reshape(TOKENS, HEADS, HDIM)
    val_cur = cur_values.astype(jnp.float32).reshape(TOKENS, HEADS, HDIM)
    key_hist = hist_keys.astype(jnp.float32).reshape(HISTORY, HEADS, HDIM)
    val_hist = hist_values.astype(jnp.float32).reshape(HISTORY, HEADS, HDIM)
    reader_ids = jnp.arange(READERS, dtype=jnp.int32)
    routed = jnp.any(piece_readers[None, :, :] == reader_ids[:, None, None], axis=2)
    key_masks = jnp.repeat(routed, PIECE, axis=1)

    def one_block(pair):
        query_rows, live_keys = pair
        query_f = query_rows.astype(jnp.float32)
        score_cur = jnp.einsum('qhd,khd->hqk', query_f, key_cur) * scale
        score_hist = jnp.einsum('qhd,khd->hqk', query_f, key_hist) * scale
        score_hist = jnp.where(live_keys[None, None, :], score_hist, -1e+30)
        row_max = jnp.maximum(lax.optimization_barrier(jnp.max(score_cur, axis=-1)), lax.optimization_barrier(jnp.max(score_hist, axis=-1)))
        expo_cur = jnp.exp(score_cur - row_max[..., None])
        expo_hist = jnp.where(live_keys[None, None, :], jnp.exp(score_hist - row_max[..., None]), 0.0)
        total = lax.optimization_barrier(jnp.sum(expo_cur, axis=-1)) + lax.optimization_barrier(jnp.sum(expo_hist, axis=-1))
        weight_cur = lax.optimization_barrier(expo_cur.astype(jnp.bfloat16)).astype(jnp.float32)
        weight_hist = lax.optimization_barrier(expo_hist.astype(jnp.bfloat16)).astype(jnp.float32)
        summed = jnp.einsum('hqk,khd->qhd', weight_cur, val_cur) + jnp.einsum('hqk,khd->qhd', weight_hist, val_hist)
        result = summed / jnp.transpose(total)[:, :, None]
        return result.astype(jnp.bfloat16).reshape(TOK_DEV, D)
    attended = lax.map(one_block, (query_blocks, key_masks)).reshape(TOKENS, D)
    return jnp.dot(attended, out_weight, preferred_element_type=jnp.float32).astype(jnp.bfloat16)
```

```python
import functools
import math

import jax
import jax.numpy as jnp
from jax import lax
from jax.experimental import pallas as pl
from jax.experimental.pallas import tpu as pltpu
from jax.sharding import PartitionSpec as P

HDIM = 128
PLANES = 8
GROUP = 4
ROWS = 192
HIST = 448
PIECE = 32
HELD = 14
YS = 4
COEF = math.log2(math.e) / math.sqrt(HDIM)
NEG = -1e30
CHUNKS = ((0, 5),)
OFFS = (4, 3, -3, 2, -2, 1, -1, 0)
BF = jnp.bfloat16
F32 = jnp.float32
ROUTE_V = ROWS
HIST_K = 2 * ROWS
HIST_V = 2 * ROWS + HIST


def seq_move(value, to):
    perm = []
    for z in range(PLANES):
        for x in range(2):
            for c in range(2):
                nz, nx, nc = to(z, x, c)
                perm.append((z * 4 + x * 2 + c, (nz % PLANES) * 4 + nx * 2 + nc))
    return lax.ppermute(value, "seq", perm)


def swap_core(value):
    return seq_move(value, lambda z, x, c: (z, x, 1 - c))


def swap_x(value):
    return seq_move(value, lambda z, x, c: (z, 1 - x, c))


def up(value):
    return seq_move(value, lambda z, x, c: (z + 1, x, c))


def down(value):
    return seq_move(value, lambda z, x, c: (z - 1, x, c))


def away(value):
    return seq_move(value, lambda z, x, c: (z + 1 - 2 * c, x, c))


def head_move(value, by_x, by_y):
    perm = []
    for x in range(2):
        for y in range(YS):
            perm.append((x * YS + y, ((x + by_x) % 2) * YS + (y + by_y) % YS))
    return lax.ppermute(value, "head", perm)


def attend_kernel(heads, first, *refs):
    table, bias = refs[0], refs[1]
    queries = refs[2:10]
    sources = refs[10:12]
    pos = 12
    if not first:
        prev_out, prev_stat = refs[pos : pos + 8], refs[pos + 8 : pos + 16]
        pos += 16
    outs, stats = refs[pos : pos + 8], refs[pos + 8 : pos + 16]
    scratch = refs[pos + 16]
    lane = lax.broadcasted_iota(jnp.int32, (ROWS, HDIM), 1)
    scratch[...] = jnp.zeros(scratch.shape, F32)

    def one_head(h, carry):
        cols = pl.ds(pl.multiple_of(h * HDIM, HDIM), HDIM)
        keys = jnp.concatenate([s[0:ROWS, cols] for s in sources], axis=0)
        vals = jnp.concatenate([s[ROWS : 2 * ROWS, cols] for s in sources], axis=0)
        for j in range(8):
            picks = [table[j, t] for t in range(4)]
            hist_k = [
                sources[t // 2][pl.ds(pl.multiple_of(HIST_K + picks[t] * PIECE, PIECE), PIECE), cols]
                for t in range(4)
            ]
            hist_v = [
                sources[t // 2][pl.ds(pl.multiple_of(HIST_V + picks[t] * PIECE, PIECE), PIECE), cols]
                for t in range(4)
            ]
            all_k = jnp.concatenate([keys] + hist_k, axis=0)
            all_v = jnp.concatenate([vals] + hist_v, axis=0)
            score = lax.dot_general(
                queries[j][:, cols], all_k, (((1,), (1,)), ((), ())), preferred_element_type=F32
            )
            score = jnp.concatenate(
                [score[:, : 2 * ROWS], score[:, 2 * ROWS :] + bias[j : j + 1, :]], axis=1
            )
            top = jnp.max(score, axis=1, keepdims=True) * COEF
            if not first:
                before = prev_stat[j][...]
                before = jnp.sum(jnp.where(lane == h, before, 0.0), axis=1, keepdims=True)
                top = jnp.maximum(top, before)
            weight = jnp.exp2(score * COEF - top)
            total = jnp.sum(weight, axis=1, keepdims=True)
            num = jnp.dot(weight.astype(BF), all_v, preferred_element_type=F32)
            if not first:
                keep = jnp.exp2(before - top)
                total = total + keep
                num = num + prev_out[j][:, cols] * keep
            num = num / total
            outs[j][:, cols] = num.astype(outs[j].dtype)
            level = top + jnp.log2(total)
            scratch[j, 0:ROWS, :] = jnp.where(lane == h, level, scratch[j, 0:ROWS, :])
        return carry

    lax.fori_loop(0, heads, one_head, 0)
    for j in range(8):
        if first:
            stats[j][...] = scratch[j, 0:ROWS, :]
        else:
            stats[j][...] = jnp.transpose(scratch[j])[0:8, :]


def attend(heads, table, bias, queries, sources, before):
    first = before is None
    width = heads * HDIM
    vmem = pl.BlockSpec(memory_space=pltpu.VMEM)
    smem = pl.BlockSpec(memory_space=pltpu.SMEM)
    args = [table, bias, *queries, *sources]
    if not first:
        args += [*before[0], *before[1]]
    out_type = F32 if first else BF
    stat_shape = (ROWS, HDIM) if first else (8, 256)
    shapes = [jax.ShapeDtypeStruct((ROWS, width), out_type)] * 8
    shapes += [jax.ShapeDtypeStruct(stat_shape, F32)] * 8
    keys = 2 * ROWS + 4 * PIECE
    result = pl.pallas_call(
        functools.partial(attend_kernel, heads, first),
        out_shape=shapes,
        in_specs=[smem] + [vmem] * (len(args) - 1),
        out_specs=[vmem] * 16,
        scratch_shapes=[pltpu.VMEM((8, 256, HDIM), F32)],
        compiler_params=pltpu.CompilerParams(vmem_limit_bytes=48 * 1024 * 1024),
        cost_estimate=pl.CostEstimate(
            flops=8 * heads * ROWS * keys * HDIM * 4,
            bytes_accessed=8 * ROWS * width * 6,
            transcendentals=8 * heads * ROWS * keys,
        ),
    )(*args)
    return result[:8], result[8:]


def blend(levels):
    top = functools.reduce(jnp.maximum, levels)
    parts = [jnp.exp2(v - top) for v in levels]
    total = functools.reduce(jnp.add, parts)
    shares = [p / total for p in parts]
    pad = jnp.zeros((HDIM - 8 * len(shares), 256), F32)
    columns = jnp.transpose(jnp.concatenate(shares + [pad], axis=0))
    return columns, top + jnp.log2(total)


def write_blend(heads, values, levels, out, stat):
    columns, level = blend(levels)
    for h in range(heads):
        cols = slice(h * HDIM, (h + 1) * HDIM)
        acc = None
        for i, v in enumerate(values):
            part = v[:, cols].astype(F32) * columns[0:ROWS, 8 * i + h : 8 * i + h + 1]
            acc = part if acc is None else acc + part
        out[:, cols] = acc.astype(BF)
    if stat is not None:
        stat[...] = level


def first_merge_kernel(heads, core, far_o, far_s, up_o, up_s, dn_o, dn_s, ou, su, od, sd):
    on_up = core[0] == 0
    far = far_s[...]
    low = jnp.full(far.shape, NEG, F32)
    write_blend(heads, [far_o, up_o], [jnp.where(on_up, far, low), up_s[...]], ou, su)
    write_blend(heads, [far_o, dn_o], [jnp.where(on_up, low, far), dn_s[...]], od, sd)


def merge_kernel(heads, ru_o, ru_s, rd_o, rd_s, up_o, up_s, dn_o, dn_s, ou, su, od, sd):
    write_blend(heads, [ru_o, up_o], [ru_s[...], up_s[...]], ou, su)
    write_blend(heads, [rd_o, dn_o], [rd_s[...], dn_s[...]], od, sd)


def last_merge_kernel(heads, ru_o, ru_s, rd_o, rd_s, own_o, own_s, out):
    write_blend(heads, [ru_o, rd_o, own_o], [ru_s[...], rd_s[...], own_s[...]], out, None)


def small_call(kernel, heads, args, pairs, scalar=False):
    width = heads * HDIM
    vmem = pl.BlockSpec(memory_space=pltpu.VMEM)
    smem = pl.BlockSpec(memory_space=pltpu.SMEM)
    value = jax.ShapeDtypeStruct((ROWS, width), BF)
    stat = jax.ShapeDtypeStruct((8, 256), F32)
    shapes = [value, stat] * pairs if pairs else value
    specs = [vmem] * len(args)
    if scalar:
        specs[0] = smem
    return pl.pallas_call(
        functools.partial(kernel, heads),
        out_shape=shapes,
        in_specs=specs,
        out_specs=[vmem] * (2 * pairs) if pairs else vmem,
        compiler_params=pltpu.CompilerParams(vmem_limit_bytes=32 * 1024 * 1024),
        cost_estimate=pl.CostEstimate(
            flops=6 * ROWS * width, bytes_accessed=12 * ROWS * width, transcendentals=8192
        ),
    )(*args)


def gather_queries(own):
    up1, dn1 = up(own), down(own)
    up2, dn2 = up(up1), down(dn1)
    up3, dn3 = up(up2), down(dn2)
    on_up = lax.rem(lax.axis_index("seq"), 2) == 0
    far = away(jnp.where(on_up, up3, dn3))
    by_off = {0: own, -1: up1, 1: dn1, -2: up2, 2: dn2, -3: up3, 3: dn3, 4: far}
    return [by_off[o] for o in OFFS]


def send_home(heads, outs, stats):
    at = {o: i for i, o in enumerate(OFFS)}
    core = lax.rem(lax.axis_index("seq"), 2).reshape(1).astype(jnp.int32)

    def loc(o):
        return outs[at[o]], stats[at[o]]

    far_o, far_s = away(outs[at[4]]), away(stats[at[4]])
    ou, su, od, sd = small_call(
        first_merge_kernel, heads, [core, far_o, far_s, *loc(3), *loc(-3)], 2, scalar=True
    )
    for o in (2, 1):
        ru_o, ru_s, rd_o, rd_s = up(ou), up(su), down(od), down(sd)
        ou, su, od, sd = small_call(
            merge_kernel, heads, [ru_o, ru_s, rd_o, rd_s, *loc(o), *loc(-o)], 2
        )
    ru_o, ru_s, rd_o, rd_s = up(ou), up(su), down(od), down(sd)
    return small_call(last_merge_kernel, heads, [ru_o, ru_s, rd_o, rd_s, *loc(0)], 0)


def routes(readers_of, me):
    blocks = jnp.stack([lax.rem(me + 4 * o + 32, 32) for o in OFFS]).astype(jnp.int32)
    tables, biases = [], []
    order = jnp.arange(HELD, dtype=jnp.int32)
    for pair in readers_of:
        picks, live = [], []
        for readers in pair:
            hit = jnp.any(readers[None, :, :] == blocks[:, None, None], axis=2)
            first = jnp.min(jnp.where(hit, order[None, :], HELD), axis=1)
            last = jnp.max(jnp.where(hit, order[None, :], -1), axis=1)
            picks += [jnp.minimum(first, HELD - 1), jnp.maximum(last, 0)]
            live += [last >= 0, last > first]
        tables.append(jnp.stack(picks, axis=1).astype(jnp.int32))
        alive = jnp.stack(live, axis=1)
        biases.append(jnp.repeat(jnp.where(alive, 0.0, NEG).astype(F32), PIECE, axis=1))
    return tables, biases


def weight_blocks(out_weight, core, y):
    mine, other = [], []
    for r in range(YS):
        target = lax.rem(y + r, YS)
        if r == 0:
            mine.append(lax.dynamic_slice_in_dim(out_weight, (core * YS + y) * 640, 640, 1))
            other.append(lax.dynamic_slice_in_dim(out_weight, ((1 - core) * YS + y) * 640, 640, 1))
        else:
            piece = lax.dynamic_slice_in_dim(out_weight, (core * YS + target) * 640, 640, 1)
            piece = head_move(piece, 0, r)
            mine.append(piece)
            other.append(swap_core(piece))
    return mine, other


def local(queries, cur_keys, cur_values, hist_keys, hist_values, piece_readers, out_weight):
    me = lax.axis_index("seq")
    core = lax.rem(me, 2)
    spot = lax.axis_index("head")
    y, x_hi = lax.rem(spot, YS), spot // YS
    readers_c = swap_core(piece_readers)
    readers_x = swap_x(piece_readers)
    readers_xc = swap_core(readers_x)
    tables, biases = routes(((piece_readers, readers_c), (readers_x, readers_xc)), me)
    mine, other = weight_blocks(out_weight, core, y)
    total_mine = total_other = None
    for h0, heads in CHUNKS:
        cols = slice(h0 * HDIM, (h0 + heads) * HDIM)
        own = jnp.concatenate(
            [cur_keys[:, cols], cur_values[:, cols], hist_keys[:, cols], hist_values[:, cols]], axis=0
        )
        own_x = swap_x(own)
        own_c = swap_core(own)
        own_xc = swap_core(own_x)
        asked = gather_queries(queries[:, cols])
        near = attend(heads, tables[0], biases[0], asked, (own, own_c), None)
        outs, stats = attend(heads, tables[1], biases[1], asked, (own_x, own_xc), near)
        attended = send_home(heads, outs, stats)
        for r in range(YS):
            part = attended if r == 0 else head_move(attended, 0, r)
            a = jnp.dot(part, mine[r][cols], preferred_element_type=F32)
            b = jnp.dot(part, other[r][cols], preferred_element_type=F32)
            total_mine = a if total_mine is None else total_mine + a
            total_other = b if total_other is None else total_other + b
    keeps = core == x_hi
    keep = jnp.where(keeps, total_mine, total_other)
    send = jnp.where(keeps, total_other, total_mine).astype(BF)
    return (keep + head_move(send, 1, 0).astype(F32)).astype(BF)


def solution(mesh):
    placed = (
        P("seq", "head"),
        P("seq", "head"),
        P("seq", "head"),
        P("seq", "head"),
        P("seq", "head"),
        P("seq", None),
        P("head", None),
    )
    return jax.shard_map(
        local, mesh=mesh, in_specs=placed, out_specs=P("seq", "head"), check_vma=False
    )
```

```python
import functools
import math

import jax
import jax.numpy as jnp
from jax import lax
from jax.experimental import pallas as pl
from jax.experimental.pallas import tpu as pltpu
from jax.sharding import PartitionSpec as P

HDIM = 128
HEADS = 5
PLANES = 8
ROWS = 192
EXTRA = 16
HIST = 448
TAIL = 2 * (ROWS + HIST)
HELD_ROWS = TAIL + 16
PIECE = 32
HELD = 14
YS = 4
HIST_K = 2 * ROWS
HIST_V = 2 * ROWS + HIST
WIDTH = HEADS * HDIM
COEF = math.log2(math.e) / math.sqrt(HDIM)
NEG = -1e30
GROUPS = (((0, 0), (0, 1), (1, 1)), ((0, 2), (1, 2)), ((0, 3), (1, 3), (0, 4)))
BLOCKS = tuple(b for g in GROUPS for b in g)
BF = jnp.bfloat16
F32 = jnp.float32
NT = (((1,), (1,)), ((), ()))
VMEM = pl.BlockSpec(memory_space=pltpu.VMEM)
SMEM = pl.BlockSpec(memory_space=pltpu.SMEM)
MIB = 1024 * 1024
SMALL = pl.CostEstimate(flops=1000, bytes_accessed=1000, transcendentals=0)
ANY = pl.BlockSpec(memory_space=pl.ANY)


def seq_move(value, to):
    perm = []
    for z in range(PLANES):
        for x in range(2):
            for c in range(2):
                nz, nx, nc = to(z, x, c)
                perm.append((z * 4 + x * 2 + c, (nz % PLANES) * 4 + nx * 2 + nc))
    return lax.ppermute(value, "seq", perm)


def swap_core(value):
    return seq_move(value, lambda z, x, c: (z, x, 1 - c))


def swap_x(value):
    return seq_move(value, lambda z, x, c: (z, 1 - x, c))


def away(value):
    return seq_move(value, lambda z, x, c: (z + 1 - 2 * c, x, c))


def home(value):
    return seq_move(value, lambda z, x, c: (z - 1 + 2 * c, x, c))


def swap_x_hi(value):
    return lax.ppermute(value, "head", [(i, (i + YS) % (2 * YS)) for i in range(2 * YS)])


def y_move(value, sign):
    perm = []
    for s in range(PLANES * 4):
        for x in range(2):
            for y in range(YS):
                to = (y + sign * (1 - 2 * (s % 2))) % YS
                perm.append(((s * 2 + x) * YS + y, (s * 2 + x) * YS + to))
    return lax.ppermute(value, ("seq", "head"), perm)


def after(value, *others):
    return lax.optimization_barrier((value, *others))[0]


def call(kernel, shapes, specs, args, mib=12, **more):
    return pl.pallas_call(
        kernel,
        out_shape=shapes,
        in_specs=specs,
        compiler_params=pltpu.CompilerParams(vmem_limit_bytes=mib * MIB),
        cost_estimate=SMALL,
        **more,
    )(*args)


def pack_kernel(cur_k, cur_v, hist_k, hist_v, readers, out, sems):
    rows = ((cur_k, 0, ROWS), (cur_v, ROWS, ROWS), (hist_k, HIST_K, HIST), (hist_v, HIST_V, HIST))
    copies = [
        pltpu.make_async_copy(ref, out.at[pl.ds(at, size), :], sems.at[i])
        for i, (ref, at, size) in enumerate(rows)
    ]
    for copy in copies:
        copy.start()
    named = readers[...].astype(F32)
    named = jnp.concatenate([named, jnp.zeros((2, WIDTH - HELD), F32)], axis=1)
    named = jnp.concatenate([named, jnp.zeros((14, WIDTH), F32)], axis=0)
    out[TAIL:HELD_ROWS, :] = named.astype(BF)
    for copy in copies:
        copy.wait()


def pack(*raw):
    return call(
        pack_kernel,
        jax.ShapeDtypeStruct((HELD_ROWS, WIDTH), BF),
        [ANY] * 4 + [VMEM],
        raw,
        mib=60,
        out_specs=VMEM,
        scratch_shapes=[pltpu.SemaphoreType.DMA((4,))],
    )


def keys_of(sources, cols, start, count):
    return [s[start : start + count, cols] for s in sources]


def pieces_of(sources, cols, start, table, j):
    found = []
    for t in range(4):
        at = pl.multiple_of(start + table[j, t] * PIECE, PIECE)
        found.append(sources[t // 2][pl.ds(at, PIECE), cols])
    return found


def biases_of(table, base, count):
    slot = lax.broadcasted_iota(jnp.int32, (1, 4 * PIECE), 1) >> 5
    rows = []
    for j in range(base, base + count):
        row = jnp.zeros((1, 4 * PIECE), F32)
        for t in range(4):
            row = jnp.where(slot == t, (1 - table[j, 4 + t]).astype(F32) * NEG, row)
        rows.append(row)
    return rows


def scores_of(query, sources, cols, table, bias, j):
    own = 2 * ROWS
    keys = keys_of(sources, cols, 0, ROWS) + pieces_of(sources, cols, HIST_K, table, j)
    score = lax.dot_general(query, jnp.concatenate(keys, axis=0), NT, preferred_element_type=F32)
    score = score * COEF
    return jnp.concatenate([score[:, :own], score[:, own:] + bias], axis=1)


def weigh(weight, sources, cols, table, j):
    vals = keys_of(sources, cols, ROWS, ROWS) + pieces_of(sources, cols, HIST_V, table, j)
    vals = jnp.concatenate(vals, axis=0)
    vals = jnp.concatenate([vals, jnp.ones(vals.shape, BF)], axis=1)
    return jnp.dot(weight.astype(BF), vals, preferred_element_type=F32)


def near_kernel(base, count, table, *refs):
    queries, sources = refs[:count], refs[count : count + 2]
    out, stat = refs[count + 2 :]
    lane = lax.broadcasted_iota(jnp.int32, (ROWS, HDIM), 1)
    stat[...] = jnp.zeros(stat.shape, F32)
    bias = biases_of(table, base, count)
    for h in range(HEADS):
        cols = slice(h * HDIM, (h + 1) * HDIM)
        for j in range(count):
            score = scores_of(queries[j][:, cols], sources, cols, table, bias[j], base + j)
            top = jnp.max(score, axis=1, keepdims=True)
            num = weigh(jnp.exp2(score - top), sources, cols, table, base + j)
            total = num[:, HDIM:]
            out[j, :, cols] = num[:, :HDIM] / total
            stat[j] = jnp.where(lane == h, top + jnp.log2(total), stat[j])


def near_pass(base, table, queries, sources):
    count = len(queries)
    return call(
        functools.partial(near_kernel, base, count),
        [
            jax.ShapeDtypeStruct((count, ROWS, WIDTH), F32),
            jax.ShapeDtypeStruct((count, ROWS, HDIM), F32),
        ],
        [SMEM] + [VMEM] * (count + 2),
        (table, *queries, *sources),
        out_specs=[VMEM, VMEM],
    )


def split3(value):
    hi = value.astype(BF).astype(F32)
    mid = (value - hi).astype(BF).astype(F32)
    return [hi, mid, value - hi - mid]


def write_level(out, level):
    tile = jnp.concatenate(split3(level) + [jnp.zeros((EXTRA - 3 * HEADS, 256), F32)], axis=0)
    tile = jnp.concatenate([tile, jnp.zeros((EXTRA, WIDTH - 256), F32)], axis=1)
    out[ROWS : ROWS + EXTRA, :] = tile.astype(BF)


def read_level(ref):
    tile = ref[ROWS : ROWS + EXTRA, 0:256].astype(F32)
    return tile[:HEADS] + tile[HEADS : 2 * HEADS] + tile[2 * HEADS : 3 * HEADS]


def far_kernel(base, count, table, *refs):
    queries, (state, level), sources = refs[:count], refs[count : count + 2], refs[count + 2 : count + 4]
    outs, stat = refs[count + 4 : 2 * count + 4], refs[2 * count + 4]
    lane = lax.broadcasted_iota(jnp.int32, (ROWS, HDIM), 1)
    stat[...] = jnp.zeros(stat.shape, F32)
    bias = biases_of(table, base, count)
    for h in range(HEADS):
        cols = slice(h * HDIM, (h + 1) * HDIM)
        for j in range(count):
            score = scores_of(queries[j][:, cols], sources, cols, table, bias[j], base + j)
            before = jnp.where(lane == h, level[j], 0.0)
            before = jnp.sum(before, axis=1, keepdims=True)
            top = jnp.maximum(jnp.max(score, axis=1, keepdims=True), before)
            num = weigh(jnp.exp2(score - top), sources, cols, table, base + j)
            keep = jnp.exp2(before - top)
            total = num[:, HDIM:] + keep
            num = (num[:, :HDIM] + state[j, :, cols] * keep) / total
            outs[j][0:ROWS, cols] = num.astype(BF)
            stat[j, 0:ROWS, :] = jnp.where(lane == h, top + jnp.log2(total), stat[j, 0:ROWS, :])
    for j in range(count):
        write_level(outs[j], jnp.transpose(stat[j])[0:HEADS, :])


def far_pass(base, table, queries, states, sources):
    count = len(queries)
    return call(
        functools.partial(far_kernel, base, count),
        [jax.ShapeDtypeStruct((ROWS + EXTRA, WIDTH), BF)] * count,
        [SMEM] + [VMEM] * (count + 4),
        (table, *queries, *states, *sources),
        out_specs=[VMEM] * count,
        scratch_shapes=[pltpu.VMEM((count, 256, HDIM), F32)],
    )


def merge_kernel(last, *refs):
    refs, out = refs[:-1], refs[-1]
    levels = [read_level(r) for r in refs]
    top = functools.reduce(jnp.maximum, levels)
    shares = [jnp.exp2(v - top) for v in levels]
    total = functools.reduce(jnp.add, shares)
    rest = jnp.zeros((8 - HEADS, 256), F32)
    stacked = []
    for s in shares:
        stacked += [s / total, rest]
    stacked.append(jnp.zeros((HDIM - 8 * len(refs), 256), F32))
    columns = jnp.transpose(jnp.concatenate(stacked, axis=0))
    for h in range(HEADS):
        cols = slice(h * HDIM, (h + 1) * HDIM)
        acc = None
        for i, ref in enumerate(refs):
            at = 8 * i + h
            part = ref[0:ROWS, cols].astype(F32) * columns[0:ROWS, at : at + 1]
            acc = part if acc is None else acc + part
        out[0:ROWS, cols] = acc.astype(BF)
    if not last:
        write_level(out, top + jnp.log2(total))


def merge(*args, last=False):
    return call(
        functools.partial(merge_kernel, last),
        jax.ShapeDtypeStruct((ROWS if last else ROWS + EXTRA, WIDTH), BF),
        [VMEM] * len(args),
        args,
        mib=6,
        out_specs=VMEM,
    )


def send_home(part, three, two):
    own = merge(home(part[0, 4]), part[0, 3])
    other = merge(home(part[1, 3]), part[1, 2])
    own = merge(home(own), after(part[0, 2], three))
    other = merge(home(other), part[1, 1])
    own = merge(home(own), after(part[0, 1], two))
    other = swap_core(home(other))
    return merge(home(own), other, part[0, 0], last=True)


def project_kernel(count, last, *refs):
    values, mine, other = refs[:count], refs[count : 2 * count], refs[2 * count : 3 * count]
    refs = refs[3 * count :]
    sums = []
    for weights in (mine, other):
        acc = None
        for v, w in zip(values, weights, strict=True):
            part = jnp.dot(v[...], w[...], preferred_element_type=F32)
            acc = part if acc is None else acc + part
        sums.append(acc)
    if last:
        flag, before_mine, before_other, keep, send = refs
        sums = [sums[0] + before_mine[...], sums[1] + before_other[...]]
        same = flag[0] == 1
        keep[...] = jnp.where(same, sums[0], sums[1])
        send[...] = jnp.where(same, sums[1], sums[0]).astype(BF)
    else:
        refs[0][...], refs[1][...] = sums


def project(values, mine, other, more=()):
    last, count = bool(more), len(values)
    specs = [VMEM] * (3 * count) + ([SMEM, VMEM, VMEM] if last else [])
    return call(
        functools.partial(project_kernel, count, last),
        [
            jax.ShapeDtypeStruct((ROWS, WIDTH), F32),
            jax.ShapeDtypeStruct((ROWS, WIDTH), BF if last else F32),
        ],
        specs,
        (*values, *mine, *other, *more),
        out_specs=[VMEM] * 2,
    )


def gather_queries(queries):
    asked = {(0, 0): queries, (1, 0): swap_core(queries)}
    for k in range(1, 5):
        for side in range(2 if k < 4 else 1):
            asked[side, k] = away(asked[side, k - 1])
    return asked


def route_kernel(place, first, second, out):
    me = place[0]
    core = me & 1
    lane = lax.broadcasted_iota(jnp.int32, (8, HDIM), 1)
    row = lax.broadcasted_iota(jnp.int32, (8, HDIM), 0)
    piece = lane.astype(F32)
    wanted = jnp.zeros((8, HDIM), jnp.int32)
    for j, (side, k) in enumerate(BLOCKS):
        column = me + side * (1 - 2 * core)
        wanted = jnp.where(row == j, (column + 4 * k * (2 * core - 1)) & 31, wanted)
    wanted = wanted.astype(F32)
    found = jnp.zeros((8, HDIM), F32)
    for g, tail in enumerate((first, second)):
        readers = tail[...].astype(F32)
        hit = (readers[0:1, :] == wanted) | (readers[1:2, :] == wanted)
        hit = hit & (lane < HELD)
        low = jnp.min(jnp.where(hit, piece, HELD), axis=1, keepdims=True)
        high = jnp.max(jnp.where(hit, piece, -1.0), axis=1, keepdims=True)
        found = jnp.where(lane == 2 * g, jnp.minimum(low, HELD - 1.0), found)
        found = jnp.where(lane == 2 * g + 1, jnp.maximum(high, 0.0), found)
        found = jnp.where(lane == 2 * g + 4, jnp.where(high >= 0.0, 1.0, 0.0), found)
        found = jnp.where(lane == 2 * g + 5, jnp.where(high > low, 1.0, 0.0), found)
    out[...] = found.astype(jnp.int32)


def routes(place, first, second):
    return call(
        route_kernel,
        jax.ShapeDtypeStruct((8, HDIM), jnp.int32),
        [SMEM, VMEM, VMEM],
        (place, first[TAIL:, :HDIM], second[TAIL:, :HDIM]),
        mib=4,
        out_specs=VMEM,
    )


def local(queries, cur_keys, cur_values, hist_keys, hist_values, piece_readers, out_weight):
    me = lax.axis_index("seq")
    core = lax.rem(me, 2)
    spot = lax.axis_index("head")
    y, x_hi = lax.rem(spot, YS), spot // YS
    place = me.reshape(1).astype(jnp.int32)

    def piece(half, r):
        start = (half * YS + lax.rem(y + r + YS, YS)) * WIDTH
        return lax.dynamic_slice_in_dim(out_weight, start, WIDTH, 1)

    held = pack(cur_keys, cur_values, hist_keys, hist_values, piece_readers.T)
    held_x = swap_x(held)
    asked = gather_queries(queries)
    held_c = swap_core(held)
    step = 1 - 2 * core
    relay = y_move(piece(core, 2), 1)
    table = routes(place, held, held_c)
    lined = [[asked[b] for b in group] for group in GROUPS]
    states = [near_pass(0, table, lined[0], (held, held_c))]
    ready = after(table, relay, states[0][0])
    states.append(near_pass(3, ready, lined[1], (held, held_c)))
    one = y_move(after(piece(core, step), relay), 1)
    ready = after(table, one, states[1][0])
    states.append(near_pass(5, ready, lined[2], (held, held_c)))
    held_xc = swap_core(after(held_x, states[2][0]))
    three = y_move(after(piece(core, -step), one), -1)
    two = y_move(after(relay, one), 1)
    table = routes(place, held_x, held_xc)
    part = {}
    for g, base in ((2, 5), (1, 3), (0, 0)):
        outs = far_pass(base, table, lined[g], states[g], (held_x, held_xc))
        part.update(zip(GROUPS[g], outs, strict=True))
    attended = send_home(part, three, two)
    mine = [piece(core, 0), one, three, two]
    other = [piece(1 - core, 0)] + [swap_core(w) for w in (three, one, two)]
    near_y, far_y = y_move(attended, 1), y_move(attended, -1)
    across = y_move(near_y, 1)
    sums = project([attended, near_y, far_y], mine[:3], other[:3])
    flag = (core == x_hi).reshape(1).astype(jnp.int32)
    keep, send = project([across], mine[3:], other[3:], (flag, *sums))
    return (keep + swap_x_hi(send).astype(F32)).astype(BF)


def solution(mesh):
    placed = (
        P("seq", "head"),
        P("seq", "head"),
        P("seq", "head"),
        P("seq", "head"),
        P("seq", "head"),
        P("seq", None),
        P("head", None),
    )
    return jax.shard_map(
        local, mesh=mesh, in_specs=placed, out_specs=P("seq", "head"), check_vma=False
    )
```

```python
import functools
import math

import jax
import jax.numpy as jnp
from jax import lax
from jax.experimental import pallas as pl
from jax.experimental.pallas import tpu as pltpu
from jax.sharding import PartitionSpec as P

HDIM = 128
HEADS = 5
PLANES = 8
ROWS = 192
EXTRA = 16
HIST = 448
TAIL = 2 * (ROWS + HIST)
HELD_ROWS = TAIL + 16
PIECE = 32
HELD = 14
YS = 4
HIST_K = 2 * ROWS
HIST_V = 2 * ROWS + HIST
WIDTH = HEADS * HDIM
COEF = math.log2(math.e) / math.sqrt(HDIM)
NEG = -1e30
GROUPS = (((0, 0), (0, 1), (1, 1)), ((0, 2), (1, 2)), ((0, 3), (1, 3), (0, 4)))
BLOCKS = tuple(b for g in GROUPS for b in g)
BF = jnp.bfloat16
F32 = jnp.float32
NT = (((1,), (1,)), ((), ()))
VMEM = pl.BlockSpec(memory_space=pltpu.VMEM)
SMEM = pl.BlockSpec(memory_space=pltpu.SMEM)
MIB = 1024 * 1024
SMALL = pl.CostEstimate(flops=1000, bytes_accessed=1000, transcendentals=0)
ANY = pl.BlockSpec(memory_space=pl.ANY)


def seq_move(value, to):
    perm = []
    for z in range(PLANES):
        for x in range(2):
            for c in range(2):
                nz, nx, nc = to(z, x, c)
                perm.append((z * 4 + x * 2 + c, (nz % PLANES) * 4 + nx * 2 + nc))
    return lax.ppermute(value, "seq", perm)


def swap_core(value):
    return seq_move(value, lambda z, x, c: (z, x, 1 - c))


def swap_x(value):
    return seq_move(value, lambda z, x, c: (z, 1 - x, c))


def away(value):
    return seq_move(value, lambda z, x, c: (z + 1 - 2 * c, x, c))


def home(value):
    return seq_move(value, lambda z, x, c: (z - 1 + 2 * c, x, c))


def swap_x_hi(value):
    return lax.ppermute(value, "head", [(i, (i + YS) % (2 * YS)) for i in range(2 * YS)])


def y_move(value, sign):
    perm = []
    for s in range(PLANES * 4):
        for x in range(2):
            for y in range(YS):
                to = (y + sign * (1 - 2 * (s % 2))) % YS
                perm.append(((s * 2 + x) * YS + y, (s * 2 + x) * YS + to))
    return lax.ppermute(value, ("seq", "head"), perm)


def after(value, *others):
    return lax.optimization_barrier((value, *others))[0]


def call(kernel, shapes, specs, args, mib=12, **more):
    return pl.pallas_call(
        kernel,
        out_shape=shapes,
        in_specs=specs,
        compiler_params=pltpu.CompilerParams(vmem_limit_bytes=mib * MIB),
        cost_estimate=SMALL,
        **more,
    )(*args)


def pack_kernel(cur_k, cur_v, hist_k, hist_v, readers, out, sems):
    rows = ((cur_k, 0, ROWS), (cur_v, ROWS, ROWS), (hist_k, HIST_K, HIST), (hist_v, HIST_V, HIST))
    copies = [
        pltpu.make_async_copy(ref, out.at[pl.ds(at, size), :], sems.at[i])
        for i, (ref, at, size) in enumerate(rows)
    ]
    for copy in copies:
        copy.start()
    named = readers[...].astype(F32)
    named = jnp.concatenate([named, jnp.zeros((2, WIDTH - HELD), F32)], axis=1)
    named = jnp.concatenate([named, jnp.zeros((14, WIDTH), F32)], axis=0)
    out[TAIL:HELD_ROWS, :] = named.astype(BF)
    for copy in copies:
        copy.wait()


def pack(*raw):
    return call(
        pack_kernel,
        jax.ShapeDtypeStruct((HELD_ROWS, WIDTH), BF),
        [ANY] * 4 + [VMEM],
        raw,
        mib=60,
        out_specs=VMEM,
        scratch_shapes=[pltpu.SemaphoreType.DMA((4,))],
    )


def keys_of(sources, cols, start, count):
    return [s[start : start + count, cols] for s in sources]


def pieces_of(sources, cols, start, table, j):
    found = []
    for t in range(4):
        at = pl.multiple_of(start + table[j, t] * PIECE, PIECE)
        found.append(sources[t // 2][pl.ds(at, PIECE), cols])
    return found


def biases_of(table, base, count):
    slot = lax.broadcasted_iota(jnp.int32, (1, 4 * PIECE), 1) >> 5
    rows = []
    for j in range(base, base + count):
        row = jnp.zeros((1, 4 * PIECE), F32)
        for t in range(4):
            row = jnp.where(slot == t, (1 - table[j, 4 + t]).astype(F32) * NEG, row)
        rows.append(row)
    return rows


def scores_of(query, sources, cols, table, bias, j):
    own = 2 * ROWS
    keys = keys_of(sources, cols, 0, ROWS) + pieces_of(sources, cols, HIST_K, table, j)
    score = lax.dot_general(query, jnp.concatenate(keys, axis=0), NT, preferred_element_type=F32)
    score = score * COEF
    return jnp.concatenate([score[:, :own], score[:, own:] + bias], axis=1)


def weigh(weight, sources, cols, table, j):
    vals = keys_of(sources, cols, ROWS, ROWS) + pieces_of(sources, cols, HIST_V, table, j)
    vals = jnp.concatenate(vals, axis=0)
    vals = jnp.concatenate([vals, jnp.ones(vals.shape, BF)], axis=1)
    return jnp.dot(weight.astype(BF), vals, preferred_element_type=F32)


def near_kernel(base, count, table, *refs):
    queries, sources = refs[:count], refs[count : count + 2]
    out, stat = refs[count + 2 :]
    lane = lax.broadcasted_iota(jnp.int32, (ROWS, HDIM), 1)
    stat[...] = jnp.zeros(stat.shape, F32)
    bias = biases_of(table, base, count)
    for h in range(HEADS):
        cols = slice(h * HDIM, (h + 1) * HDIM)
        for j in range(count):
            score = scores_of(queries[j][:, cols], sources, cols, table, bias[j], base + j)
            top = jnp.max(score, axis=1, keepdims=True)
            num = weigh(jnp.exp2(score - top), sources, cols, table, base + j)
            total = num[:, HDIM:]
            out[j, :, cols] = num[:, :HDIM] / total
            stat[j] = jnp.where(lane == h, top + jnp.log2(total), stat[j])


def near_pass(base, table, queries, sources):
    count = len(queries)
    return call(
        functools.partial(near_kernel, base, count),
        [
            jax.ShapeDtypeStruct((count, ROWS, WIDTH), F32),
            jax.ShapeDtypeStruct((count, ROWS, HDIM), F32),
        ],
        [SMEM] + [VMEM] * (count + 2),
        (table, *queries, *sources),
        out_specs=[VMEM, VMEM],
    )


def split3(value):
    hi = value.astype(BF).astype(F32)
    mid = (value - hi).astype(BF).astype(F32)
    return [hi, mid, value - hi - mid]


def write_level(out, level):
    tile = jnp.concatenate(split3(level) + [jnp.zeros((EXTRA - 3 * HEADS, 256), F32)], axis=0)
    tile = jnp.concatenate([tile, jnp.zeros((EXTRA, WIDTH - 256), F32)], axis=1)
    out[ROWS : ROWS + EXTRA, :] = tile.astype(BF)


def read_level(ref):
    tile = ref[ROWS : ROWS + EXTRA, 0:256].astype(F32)
    return tile[:HEADS] + tile[HEADS : 2 * HEADS] + tile[2 * HEADS : 3 * HEADS]


def far_kernel(base, count, table, *refs):
    queries, (state, level), sources = refs[:count], refs[count : count + 2], refs[count + 2 : count + 4]
    outs, stat = refs[count + 4 : 2 * count + 4], refs[2 * count + 4]
    lane = lax.broadcasted_iota(jnp.int32, (ROWS, HDIM), 1)
    stat[...] = jnp.zeros(stat.shape, F32)
    bias = biases_of(table, base, count)
    for h in range(HEADS):
        cols = slice(h * HDIM, (h + 1) * HDIM)
        for j in range(count):
            score = scores_of(queries[j][:, cols], sources, cols, table, bias[j], base + j)
            before = jnp.where(lane == h, level[j], 0.0)
            before = jnp.sum(before, axis=1, keepdims=True)
            top = jnp.maximum(jnp.max(score, axis=1, keepdims=True), before)
            num = weigh(jnp.exp2(score - top), sources, cols, table, base + j)
            keep = jnp.exp2(before - top)
            total = num[:, HDIM:] + keep
            num = (num[:, :HDIM] + state[j, :, cols] * keep) / total
            outs[j][0:ROWS, cols] = num.astype(BF)
            stat[j, 0:ROWS, :] = jnp.where(lane == h, top + jnp.log2(total), stat[j, 0:ROWS, :])
    for j in range(count):
        write_level(outs[j], jnp.transpose(stat[j])[0:HEADS, :])


def far_pass(base, table, queries, states, sources):
    count = len(queries)
    return call(
        functools.partial(far_kernel, base, count),
        [jax.ShapeDtypeStruct((ROWS + EXTRA, WIDTH), BF)] * count,
        [SMEM] + [VMEM] * (count + 4),
        (table, *queries, *states, *sources),
        out_specs=[VMEM] * count,
        scratch_shapes=[pltpu.VMEM((count, 256, HDIM), F32)],
    )


def merge_kernel(last, *refs):
    refs, out = refs[:-1], refs[-1]
    levels = [read_level(r) for r in refs]
    top = functools.reduce(jnp.maximum, levels)
    shares = [jnp.exp2(v - top) for v in levels]
    total = functools.reduce(jnp.add, shares)
    rest = jnp.zeros((8 - HEADS, 256), F32)
    stacked = []
    for s in shares:
        stacked += [s / total, rest]
    stacked.append(jnp.zeros((HDIM - 8 * len(refs), 256), F32))
    columns = jnp.transpose(jnp.concatenate(stacked, axis=0))
    for h in range(HEADS):
        cols = slice(h * HDIM, (h + 1) * HDIM)
        acc = None
        for i, ref in enumerate(refs):
            at = 8 * i + h
            part = ref[0:ROWS, cols].astype(F32) * columns[0:ROWS, at : at + 1]
            acc = part if acc is None else acc + part
        out[0:ROWS, cols] = acc.astype(BF)
    if not last:
        write_level(out, top + jnp.log2(total))


def merge(*args, last=False):
    return call(
        functools.partial(merge_kernel, last),
        jax.ShapeDtypeStruct((ROWS if last else ROWS + EXTRA, WIDTH), BF),
        [VMEM] * len(args),
        args,
        mib=6,
        out_specs=VMEM,
    )


def send_home(part):
    own = merge(home(part[0, 4]), part[0, 3])
    other = merge(home(part[1, 3]), part[1, 2])
    own = merge(home(own), part[0, 2])
    other = merge(home(other), part[1, 1])
    own = merge(home(own), part[0, 1])
    other = swap_core(home(other))
    return merge(home(own), other, part[0, 0], last=True)


def project_kernel(count, last, *refs):
    values, mine, other = refs[:count], refs[count : 2 * count], refs[2 * count : 3 * count]
    refs = refs[3 * count :]
    sums = []
    for weights in (mine, other):
        acc = None
        for v, w in zip(values, weights, strict=True):
            part = jnp.dot(v[...], w[...], preferred_element_type=F32)
            acc = part if acc is None else acc + part
        sums.append(acc)
    if last:
        flag, before_mine, before_other, keep, send = refs
        sums = [sums[0] + before_mine[...], sums[1] + before_other[...]]
        same = flag[0] == 1
        keep[...] = jnp.where(same, sums[0], sums[1])
        send[...] = jnp.where(same, sums[1], sums[0]).astype(BF)
    else:
        refs[0][...], refs[1][...] = sums


def project(values, mine, other, more=()):
    last, count = bool(more), len(values)
    specs = [VMEM] * (3 * count) + ([SMEM, VMEM, VMEM] if last else [])
    return call(
        functools.partial(project_kernel, count, last),
        [
            jax.ShapeDtypeStruct((ROWS, WIDTH), F32),
            jax.ShapeDtypeStruct((ROWS, WIDTH), BF if last else F32),
        ],
        specs,
        (*values, *mine, *other, *more),
        out_specs=[VMEM] * 2,
    )


def gather_queries(queries):
    asked = {(0, 0): queries, (1, 0): swap_core(queries)}
    for k in range(1, 5):
        for side in range(2 if k < 4 else 1):
            asked[side, k] = away(asked[side, k - 1])
    return asked


def route_kernel(place, first, second, out):
    me = place[0]
    core = me & 1
    lane = lax.broadcasted_iota(jnp.int32, (8, HDIM), 1)
    row = lax.broadcasted_iota(jnp.int32, (8, HDIM), 0)
    piece = lane.astype(F32)
    wanted = jnp.zeros((8, HDIM), jnp.int32)
    for j, (side, k) in enumerate(BLOCKS):
        column = me + side * (1 - 2 * core)
        wanted = jnp.where(row == j, (column + 4 * k * (2 * core - 1)) & 31, wanted)
    wanted = wanted.astype(F32)
    found = jnp.zeros((8, HDIM), F32)
    for g, tail in enumerate((first, second)):
        readers = tail[...].astype(F32)
        hit = (readers[0:1, :] == wanted) | (readers[1:2, :] == wanted)
        hit = hit & (lane < HELD)
        low = jnp.min(jnp.where(hit, piece, HELD), axis=1, keepdims=True)
        high = jnp.max(jnp.where(hit, piece, -1.0), axis=1, keepdims=True)
        found = jnp.where(lane == 2 * g, jnp.minimum(low, HELD - 1.0), found)
        found = jnp.where(lane == 2 * g + 1, jnp.maximum(high, 0.0), found)
        found = jnp.where(lane == 2 * g + 4, jnp.where(high >= 0.0, 1.0, 0.0), found)
        found = jnp.where(lane == 2 * g + 5, jnp.where(high > low, 1.0, 0.0), found)
    out[...] = found.astype(jnp.int32)


def routes(place, first, second):
    return call(
        route_kernel,
        jax.ShapeDtypeStruct((8, HDIM), jnp.int32),
        [SMEM, VMEM, VMEM],
        (place, first[TAIL:, :HDIM], second[TAIL:, :HDIM]),
        mib=4,
        out_specs=VMEM,
    )


def local(queries, cur_keys, cur_values, hist_keys, hist_values, piece_readers, out_weight):
    me = lax.axis_index("seq")
    core = lax.rem(me, 2)
    spot = lax.axis_index("head")
    y, x_hi = lax.rem(spot, YS), spot // YS
    place = me.reshape(1).astype(jnp.int32)

    held = pack(cur_keys, cur_values, hist_keys, hist_values, piece_readers.T)
    held_x = swap_x(held)
    asked = gather_queries(queries)
    held_c = swap_core(held)
    step = 1 - 2 * core
    spread = after(out_weight, held_c)

    def piece(half, r):
        start = (half * YS + lax.rem(y + r + YS, YS)) * WIDTH
        return lax.dynamic_slice_in_dim(spread, start, WIDTH, 1)

    relay = y_move(piece(core, 2), 1)
    table = routes(place, held, held_c)
    lined = [[asked[b] for b in group] for group in GROUPS]
    states = [near_pass(0, table, lined[0], (held, held_c))]
    ready = after(table, states[0][0])
    states.append(near_pass(3, ready, lined[1], (held, held_c)))
    one = y_move(piece(core, step), 1)
    ready = after(table, relay, one, states[1][0])
    states.append(near_pass(5, ready, lined[2], (held, held_c)))
    held_xc = swap_core(after(held_x, states[2][0]))
    three = y_move(after(piece(core, -step), asked[0, 3]), -1)
    two = y_move(after(relay, asked[0, 3]), 1)
    table = routes(place, held_x, held_xc)
    part = {}
    for g, base in ((2, 5), (1, 3), (0, 0)):
        outs = far_pass(base, table, lined[g], states[g], (held_x, held_xc))
        part.update(zip(GROUPS[g], outs, strict=True))
    part[0, 1] = after(part[0, 1], three, two)
    attended = send_home(part)
    mine = [piece(core, 0), one, three, two]
    other = [piece(1 - core, 0)] + [swap_core(w) for w in (three, one, two)]
    near_y, far_y = y_move(attended, 1), y_move(attended, -1)
    across = y_move(near_y, 1)
    sums = project([attended, near_y, far_y], mine[:3], other[:3])
    flag = (core == x_hi).reshape(1).astype(jnp.int32)
    keep, send = project([across], mine[3:], other[3:], (flag, *sums))
    return (keep + swap_x_hi(send).astype(F32)).astype(BF)


def solution(mesh):
    placed = (
        P("seq", "head"),
        P("seq", "head"),
        P("seq", "head"),
        P("seq", "head"),
        P("seq", "head"),
        P("seq", None),
        P("head", None),
    )
    return jax.shard_map(
        local, mesh=mesh, in_specs=placed, out_specs=P("seq", "head"), check_vma=False
    )
```

```python
import functools
import math

import jax
import jax.numpy as jnp
from jax import lax
from jax.experimental import pallas as pl
from jax.experimental.pallas import tpu as pltpu
from jax.sharding import PartitionSpec as P

HDIM = 128
HEADS = 5
PLANES = 8
ROWS = 192
EXTRA = 16
HIST = 448
TAIL = 2 * (ROWS + HIST)
HELD_ROWS = TAIL + 16
PIECE = 32
HELD = 14
YS = 4
HIST_K = 2 * ROWS
HIST_V = 2 * ROWS + HIST
WIDTH = HEADS * HDIM
COEF = math.log2(math.e) / math.sqrt(HDIM)
NEG = -1e30
GROUPS = (((0, 0), (0, 1), (1, 1)), ((0, 2), (1, 2)), ((0, 3), (1, 3), (0, 4)))
BLOCKS = tuple(b for g in GROUPS for b in g)
FAR = ((2, 5, 2, 1), (2, 5, 0, 2), (1, 3, 0, 2), (0, 0, 0, 3))
BF = jnp.bfloat16
F32 = jnp.float32
NT = (((1,), (1,)), ((), ()))
VMEM = pl.BlockSpec(memory_space=pltpu.VMEM)
SMEM = pl.BlockSpec(memory_space=pltpu.SMEM)
MIB = 1024 * 1024
SMALL = pl.CostEstimate(flops=1000, bytes_accessed=1000, transcendentals=0)
ANY = pl.BlockSpec(memory_space=pl.ANY)


def seq_move(value, to):
    perm = []
    for z in range(PLANES):
        for x in range(2):
            for c in range(2):
                nz, nx, nc = to(z, x, c)
                perm.append((z * 4 + x * 2 + c, (nz % PLANES) * 4 + nx * 2 + nc))
    return lax.ppermute(value, "seq", perm)


def swap_core(value):
    return seq_move(value, lambda z, x, c: (z, x, 1 - c))


def swap_x(value):
    return seq_move(value, lambda z, x, c: (z, 1 - x, c))


def away(value):
    return seq_move(value, lambda z, x, c: (z + 1 - 2 * c, x, c))


def home(value):
    return seq_move(value, lambda z, x, c: (z - 1 + 2 * c, x, c))


def swap_x_hi(value):
    return lax.ppermute(value, "head", [(i, (i + YS) % (2 * YS)) for i in range(2 * YS)])


def y_move(value, sign):
    perm = []
    for s in range(PLANES * 4):
        for x in range(2):
            for y in range(YS):
                to = (y + sign * (1 - 2 * (s % 2))) % YS
                perm.append(((s * 2 + x) * YS + y, (s * 2 + x) * YS + to))
    return lax.ppermute(value, ("seq", "head"), perm)


def after(value, *others):
    return lax.optimization_barrier((value, *others))[0]


def call(kernel, shapes, specs, args, mib=12, cost=SMALL, **more):
    return pl.pallas_call(
        kernel,
        out_shape=shapes,
        in_specs=specs,
        compiler_params=pltpu.CompilerParams(vmem_limit_bytes=mib * MIB),
        cost_estimate=cost,
        **more,
    )(*args)


def pack_kernel(cur_k, cur_v, hist_k, hist_v, readers, out, room, came, gone):
    rows = ((hist_k, HIST_K, HIST), (hist_v, HIST_V, HIST), (cur_k, 0, ROWS), (cur_v, ROWS, ROWS))
    reads, writes = [], []
    for i, (ref, at, size) in enumerate(rows):
        part = room.at[pl.ds(at, size), :]
        reads.append(pltpu.make_async_copy(ref, part, came.at[i]))
        writes.append(pltpu.make_async_copy(part, out.at[pl.ds(at, size), :], gone.at[i]))
    for read in reads:
        read.start()
    named = readers[...].astype(F32)
    named = jnp.concatenate([named, jnp.zeros((2, WIDTH - HELD), F32)], axis=1)
    named = jnp.concatenate([named, jnp.zeros((14, WIDTH), F32)], axis=0)
    room[TAIL:HELD_ROWS, :] = named.astype(BF)
    last = pltpu.make_async_copy(
        room.at[pl.ds(TAIL, 16), :], out.at[pl.ds(TAIL, 16), :], gone.at[4]
    )
    last.start()
    for read, write in zip(reads, writes, strict=True):
        read.wait()
        write.start()
    for write in writes:
        write.wait()
    last.wait()


def pack(*raw):
    return call(
        pack_kernel,
        jax.ShapeDtypeStruct((HELD_ROWS, WIDTH), BF),
        [ANY] * 4 + [VMEM],
        raw,
        mib=60,
        out_specs=ANY,
        scratch_shapes=[
            pltpu.VMEM((HELD_ROWS, WIDTH), BF),
            pltpu.SemaphoreType.DMA((4,)),
            pltpu.SemaphoreType.DMA((5,)),
        ],
    )


def keys_of(sources, cols, start, count):
    return [s[start : start + count, cols] for s in sources]


def pieces_of(sources, cols, start, table, j):
    found = []
    for t in range(4):
        at = pl.multiple_of(start + table[j, t] * PIECE, PIECE)
        found.append(sources[t // 2][pl.ds(at, PIECE), cols])
    return found


def biases_of(table, base, count):
    slot = lax.broadcasted_iota(jnp.int32, (1, 4 * PIECE), 1) >> 5
    rows = []
    for j in range(base, base + count):
        row = jnp.zeros((1, 4 * PIECE), F32)
        for t in range(4):
            row = jnp.where(slot == t, (1 - table[j, 4 + t]).astype(F32) * NEG, row)
        rows.append(row)
    return rows


def scores_of(query, sources, cols, table, bias, j):
    own = 2 * ROWS
    keys = keys_of(sources, cols, 0, ROWS) + pieces_of(sources, cols, HIST_K, table, j)
    score = lax.dot_general(query, jnp.concatenate(keys, axis=0), NT, preferred_element_type=F32)
    score = score * COEF
    return jnp.concatenate([score[:, :own], score[:, own:] + bias], axis=1)


def weigh(weight, sources, cols, table, j):
    vals = keys_of(sources, cols, ROWS, ROWS) + pieces_of(sources, cols, HIST_V, table, j)
    vals = jnp.concatenate(vals, axis=0)
    vals = jnp.concatenate([vals, jnp.ones(vals.shape, BF)], axis=1)
    return jnp.dot(weight.astype(BF), vals, preferred_element_type=F32)


def near_kernel(base, count, table, *refs):
    queries, sources = refs[:count], refs[count : count + 2]
    out, stat = refs[count + 2 :]
    lane = lax.broadcasted_iota(jnp.int32, (ROWS, HDIM), 1)
    stat[...] = jnp.zeros(stat.shape, F32)
    bias = biases_of(table, base, count)
    for h in range(HEADS):
        cols = slice(h * HDIM, (h + 1) * HDIM)
        for j in range(count):
            score = scores_of(queries[j][:, cols], sources, cols, table, bias[j], base + j)
            top = jnp.max(score, axis=1, keepdims=True)
            num = weigh(jnp.exp2(score - top), sources, cols, table, base + j)
            total = num[:, HDIM:]
            out[j, :, cols] = num[:, :HDIM] / total
            stat[j] = jnp.where(lane == h, top + jnp.log2(total), stat[j])


def near_pass(base, table, queries, sources):
    count = len(queries)
    return call(
        functools.partial(near_kernel, base, count),
        [
            jax.ShapeDtypeStruct((count, ROWS, WIDTH), F32),
            jax.ShapeDtypeStruct((count, ROWS, HDIM), F32),
        ],
        [SMEM] + [VMEM] * (count + 2),
        (table, *queries, *sources),
        out_specs=[VMEM, VMEM],
    )


def split3(value):
    hi = value.astype(BF).astype(F32)
    mid = (value - hi).astype(BF).astype(F32)
    return [hi, mid, value - hi - mid]


def write_level(out, level):
    tile = jnp.concatenate(split3(level) + [jnp.zeros((EXTRA - 3 * HEADS, 256), F32)], axis=0)
    tile = jnp.concatenate([tile, jnp.zeros((EXTRA, WIDTH - 256), F32)], axis=1)
    out[ROWS : ROWS + EXTRA, :] = tile.astype(BF)


def read_level(ref):
    tile = ref[ROWS : ROWS + EXTRA, 0:256].astype(F32)
    return tile[:HEADS] + tile[HEADS : 2 * HEADS] + tile[2 * HEADS : 3 * HEADS]


def far_kernel(base, offset, count, table, *refs):
    queries, (state, level), sources = refs[:count], refs[count : count + 2], refs[count + 2 : count + 4]
    outs, stat = refs[count + 4 : 2 * count + 4], refs[2 * count + 4]
    lane = lax.broadcasted_iota(jnp.int32, (ROWS, HDIM), 1)
    stat[...] = jnp.zeros(stat.shape, F32)
    bias = biases_of(table, base, count)
    for h in range(HEADS):
        cols = slice(h * HDIM, (h + 1) * HDIM)
        for j in range(count):
            score = scores_of(queries[j][:, cols], sources, cols, table, bias[j], base + j)
            before = jnp.where(lane == h, level[offset + j], 0.0)
            before = jnp.sum(before, axis=1, keepdims=True)
            top = jnp.maximum(jnp.max(score, axis=1, keepdims=True), before)
            num = weigh(jnp.exp2(score - top), sources, cols, table, base + j)
            keep = jnp.exp2(before - top)
            total = num[:, HDIM:] + keep
            num = (num[:, :HDIM] + state[offset + j, :, cols] * keep) / total
            outs[j][0:ROWS, cols] = num.astype(BF)
            stat[j, 0:ROWS, :] = jnp.where(lane == h, top + jnp.log2(total), stat[j, 0:ROWS, :])
    for j in range(count):
        write_level(outs[j], jnp.transpose(stat[j])[0:HEADS, :])


def far_pass(base, offset, table, queries, states, sources):
    count = len(queries)
    return call(
        functools.partial(far_kernel, base + offset, offset, count),
        [jax.ShapeDtypeStruct((ROWS + EXTRA, WIDTH), BF)] * count,
        [SMEM] + [VMEM] * (count + 4),
        (table, *queries, *states, *sources),
        out_specs=[VMEM] * count,
        scratch_shapes=[pltpu.VMEM((count, 256, HDIM), F32)],
    )


def merge_kernel(last, *refs):
    refs, out = refs[:-1], refs[-1]
    levels = [read_level(r) for r in refs]
    top = functools.reduce(jnp.maximum, levels)
    shares = [jnp.exp2(v - top) for v in levels]
    total = functools.reduce(jnp.add, shares)
    rest = jnp.zeros((8 - HEADS, 256), F32)
    stacked = []
    for s in shares:
        stacked += [s / total, rest]
    stacked.append(jnp.zeros((HDIM - 8 * len(refs), 256), F32))
    columns = jnp.transpose(jnp.concatenate(stacked, axis=0))
    for h in range(HEADS):
        cols = slice(h * HDIM, (h + 1) * HDIM)
        acc = None
        for i, ref in enumerate(refs):
            at = 8 * i + h
            part = ref[0:ROWS, cols].astype(F32) * columns[0:ROWS, at : at + 1]
            acc = part if acc is None else acc + part
        out[0:ROWS, cols] = acc.astype(BF)
    if not last:
        write_level(out, top + jnp.log2(total))


def merge(*args, last=False):
    return call(
        functools.partial(merge_kernel, last),
        jax.ShapeDtypeStruct((ROWS if last else ROWS + EXTRA, WIDTH), BF),
        [VMEM] * len(args),
        args,
        mib=6,
        out_specs=VMEM,
    )


def send_home(part):
    own = merge(home(part[0, 4]), part[0, 3])
    other = merge(home(part[1, 3]), part[1, 2])
    own = merge(home(own), part[0, 2])
    other = merge(home(other), part[1, 1])
    own = merge(home(own), part[0, 1])
    other = swap_core(home(other))
    return merge(home(own), other, part[0, 0], last=True)


def project_kernel(count, last, *refs):
    values, mine, other = refs[:count], refs[count : 2 * count], refs[2 * count : 3 * count]
    refs = refs[3 * count :]
    sums = []
    for weights in (mine, other):
        acc = None
        for v, w in zip(values, weights, strict=True):
            part = jnp.dot(v[...], w[...], preferred_element_type=F32)
            acc = part if acc is None else acc + part
        sums.append(acc)
    if last:
        flag, before_mine, before_other, keep, send = refs
        sums = [sums[0] + before_mine[...], sums[1] + before_other[...]]
        same = flag[0] == 1
        keep[...] = jnp.where(same, sums[0], sums[1])
        send[...] = jnp.where(same, sums[1], sums[0]).astype(BF)
    else:
        refs[0][...], refs[1][...] = sums


def project(values, mine, other, more=()):
    last, count = bool(more), len(values)
    specs = [VMEM] * (3 * count) + ([SMEM, VMEM, VMEM] if last else [])
    return call(
        functools.partial(project_kernel, count, last),
        [
            jax.ShapeDtypeStruct((ROWS, WIDTH), F32),
            jax.ShapeDtypeStruct((ROWS, WIDTH), BF if last else F32),
        ],
        specs,
        (*values, *mine, *other, *more),
        out_specs=[VMEM] * 2,
    )


def gather_queries(queries):
    asked = {(0, 0): queries, (1, 0): swap_core(queries)}
    for k in range(1, 5):
        for side in range(2 if k < 4 else 1):
            asked[side, k] = away(asked[side, k - 1])
    return asked


def route_kernel(place, first, second, out):
    me = place[0]
    core = me & 1
    lane = lax.broadcasted_iota(jnp.int32, (8, HDIM), 1)
    row = lax.broadcasted_iota(jnp.int32, (8, HDIM), 0)
    piece = lane.astype(F32)
    wanted = jnp.zeros((8, HDIM), jnp.int32)
    for j, (side, k) in enumerate(BLOCKS):
        column = me + side * (1 - 2 * core)
        wanted = jnp.where(row == j, (column + 4 * k * (2 * core - 1)) & 31, wanted)
    wanted = wanted.astype(F32)
    found = jnp.zeros((8, HDIM), F32)
    for g, tail in enumerate((first, second)):
        readers = tail[...].astype(F32)
        hit = (readers[0:1, :] == wanted) | (readers[1:2, :] == wanted)
        hit = hit & (lane < HELD)
        low = jnp.min(jnp.where(hit, piece, HELD), axis=1, keepdims=True)
        high = jnp.max(jnp.where(hit, piece, -1.0), axis=1, keepdims=True)
        found = jnp.where(lane == 2 * g, jnp.minimum(low, HELD - 1.0), found)
        found = jnp.where(lane == 2 * g + 1, jnp.maximum(high, 0.0), found)
        found = jnp.where(lane == 2 * g + 4, jnp.where(high >= 0.0, 1.0, 0.0), found)
        found = jnp.where(lane == 2 * g + 5, jnp.where(high > low, 1.0, 0.0), found)
    out[...] = found.astype(jnp.int32)


def routes(place, first, second):
    return call(
        route_kernel,
        jax.ShapeDtypeStruct((8, HDIM), jnp.int32),
        [SMEM, VMEM, VMEM],
        (place, first[TAIL:, :HDIM], second[TAIL:, :HDIM]),
        mib=4,
        out_specs=VMEM,
    )


def local(queries, cur_keys, cur_values, hist_keys, hist_values, piece_readers, out_weight):
    me = lax.axis_index("seq")
    core = lax.rem(me, 2)
    spot = lax.axis_index("head")
    y, x_hi = lax.rem(spot, YS), spot // YS
    place = me.reshape(1).astype(jnp.int32)

    held = pack(cur_keys, cur_values, hist_keys, hist_values, piece_readers.T)
    held_x = swap_x(held)
    asked = gather_queries(queries)
    held_c = swap_core(held)
    step = 1 - 2 * core
    spread = after(out_weight, held_c)

    def piece(half, r):
        start = (half * YS + lax.rem(y + r + YS, YS)) * WIDTH
        return lax.dynamic_slice_in_dim(spread, start, WIDTH, 1)

    relay = y_move(piece(core, 2), 1)
    table = routes(place, held, held_c)
    lined = [[asked[b] for b in group] for group in GROUPS]
    states = [near_pass(0, table, lined[0], (held, held_c))]
    ready = after(table, states[0][0])
    states.append(near_pass(3, ready, lined[1], (held, held_c)))
    one = y_move(piece(core, step), 1)
    ready = after(table, relay, one, states[1][0])
    states.append(near_pass(5, ready, lined[2], (held, held_c)))
    held_xc = swap_core(after(held_x, states[2][0]))
    three = y_move(after(piece(core, -step), asked[0, 3]), -1)
    two = y_move(after(relay, asked[0, 3]), 1)
    table = routes(place, held_x, held_xc)
    part = {}
    for g, base, offset, count in FAR:
        blocks = GROUPS[g][offset : offset + count]
        outs = far_pass(base, offset, table, [asked[b] for b in blocks], states[g], (held_x, held_xc))
        part.update(zip(blocks, outs, strict=True))
    part[0, 1] = after(part[0, 1], three, two)
    attended = send_home(part)
    mine = [piece(core, 0), one, three, two]
    other = [piece(1 - core, 0)] + [swap_core(w) for w in (three, one, two)]
    near_y, far_y = y_move(attended, 1), y_move(attended, -1)
    across = y_move(near_y, 1)
    sums = project([attended, near_y, far_y], mine[:3], other[:3])
    flag = (core == x_hi).reshape(1).astype(jnp.int32)
    keep, send = project([across], mine[3:], other[3:], (flag, *sums))
    return (keep + swap_x_hi(send).astype(F32)).astype(BF)


def solution(mesh):
    placed = (
        P("seq", "head"),
        P("seq", "head"),
        P("seq", "head"),
        P("seq", "head"),
        P("seq", "head"),
        P("seq", None),
        P("head", None),
    )
    return jax.shard_map(
        local, mesh=mesh, in_specs=placed, out_specs=P("seq", "head"), check_vma=False
    )
```

```python
import functools
import math

import jax
import jax.numpy as jnp
from jax import lax
from jax.experimental import pallas as pl
from jax.experimental.pallas import tpu as pltpu
from jax.sharding import PartitionSpec as P

HDIM = 128
HEADS = 5
PLANES = 8
ROWS = 192
EXTRA = 16
HIST = 448
TAIL = 2 * (ROWS + HIST)
HELD_ROWS = TAIL + 16
PIECE = 32
HELD = 14
YS = 4
HIST_K = 2 * ROWS
HIST_V = 2 * ROWS + HIST
WIDTH = HEADS * HDIM
COEF = math.log2(math.e) / math.sqrt(HDIM)
NEG = -1e30
GROUPS = (((0, 0), (0, 1), (1, 1)), ((0, 2), (1, 2)), ((0, 3), (1, 3), (0, 4)))
BLOCKS = tuple(b for g in GROUPS for b in g)
FAR = ((2, 5, 2, 1), (2, 5, 0, 2), (1, 3, 0, 2), (0, 0, 0, 3))
BF = jnp.bfloat16
F32 = jnp.float32
NT = (((1,), (1,)), ((), ()))
VMEM = pl.BlockSpec(memory_space=pltpu.VMEM)
SMEM = pl.BlockSpec(memory_space=pltpu.SMEM)
MIB = 1024 * 1024
SMALL = pl.CostEstimate(flops=1000, bytes_accessed=1000, transcendentals=0)
LONG = pl.CostEstimate(flops=5000000000, bytes_accessed=1000, transcendentals=0)
ANY = pl.BlockSpec(memory_space=pl.ANY)


def seq_move(value, to):
    perm = []
    for z in range(PLANES):
        for x in range(2):
            for c in range(2):
                nz, nx, nc = to(z, x, c)
                perm.append((z * 4 + x * 2 + c, (nz % PLANES) * 4 + nx * 2 + nc))
    return lax.ppermute(value, "seq", perm)


def swap_core(value):
    return seq_move(value, lambda z, x, c: (z, x, 1 - c))


def swap_x(value):
    return seq_move(value, lambda z, x, c: (z, 1 - x, c))


def away(value):
    return seq_move(value, lambda z, x, c: (z + 1 - 2 * c, x, c))


def home(value):
    return seq_move(value, lambda z, x, c: (z - 1 + 2 * c, x, c))


def swap_x_hi(value):
    return lax.ppermute(value, "head", [(i, (i + YS) % (2 * YS)) for i in range(2 * YS)])


def y_move(value, sign):
    perm = []
    for s in range(PLANES * 4):
        for x in range(2):
            for y in range(YS):
                to = (y + sign * (1 - 2 * (s % 2))) % YS
                perm.append(((s * 2 + x) * YS + y, (s * 2 + x) * YS + to))
    return lax.ppermute(value, ("seq", "head"), perm)


def after(value, *others):
    return lax.optimization_barrier((value, *others))[0]


def call(kernel, shapes, specs, args, mib=12, cost=SMALL, **more):
    return pl.pallas_call(
        kernel,
        out_shape=shapes,
        in_specs=specs,
        compiler_params=pltpu.CompilerParams(vmem_limit_bytes=mib * MIB),
        cost_estimate=cost,
        **more,
    )(*args)


def pack_kernel(cur_k, cur_v, hist_k, hist_v, readers, out, room, came, gone):
    rows = ((hist_k, HIST_K, HIST), (hist_v, HIST_V, HIST), (cur_k, 0, ROWS), (cur_v, ROWS, ROWS))
    reads, writes = [], []
    for i, (ref, at, size) in enumerate(rows):
        part = room.at[pl.ds(at, size), :]
        reads.append(pltpu.make_async_copy(ref, part, came.at[i]))
        writes.append(pltpu.make_async_copy(part, out.at[pl.ds(at, size), :], gone.at[i]))
    for read in reads:
        read.start()
    named = readers[...].astype(F32)
    named = jnp.concatenate([named, jnp.zeros((2, WIDTH - HELD), F32)], axis=1)
    named = jnp.concatenate([named, jnp.zeros((14, WIDTH), F32)], axis=0)
    room[TAIL:HELD_ROWS, :] = named.astype(BF)
    last = pltpu.make_async_copy(
        room.at[pl.ds(TAIL, 16), :], out.at[pl.ds(TAIL, 16), :], gone.at[4]
    )
    last.start()
    for read, write in zip(reads, writes, strict=True):
        read.wait()
        write.start()
    for write in writes:
        write.wait()
    last.wait()


def pack(*raw):
    return call(
        pack_kernel,
        jax.ShapeDtypeStruct((HELD_ROWS, WIDTH), BF),
        [ANY] * 4 + [VMEM],
        raw,
        mib=60,
        out_specs=ANY,
        scratch_shapes=[
            pltpu.VMEM((HELD_ROWS, WIDTH), BF),
            pltpu.SemaphoreType.DMA((4,)),
            pltpu.SemaphoreType.DMA((5,)),
        ],
    )


def keys_of(sources, cols, start, count):
    return [s[start : start + count, cols] for s in sources]


def pieces_of(sources, cols, start, table, j):
    found = []
    for t in range(4):
        at = pl.multiple_of(start + table[j, t] * PIECE, PIECE)
        found.append(sources[t // 2][pl.ds(at, PIECE), cols])
    return found


def biases_of(table, base, count):
    slot = lax.broadcasted_iota(jnp.int32, (1, 4 * PIECE), 1) >> 5
    rows = []
    for j in range(base, base + count):
        row = jnp.zeros((1, 4 * PIECE), F32)
        for t in range(4):
            row = jnp.where(slot == t, (1 - table[j, 4 + t]).astype(F32) * NEG, row)
        rows.append(row)
    return rows


def scores_of(query, sources, cols, table, bias, j):
    own = 2 * ROWS
    keys = keys_of(sources, cols, 0, ROWS) + pieces_of(sources, cols, HIST_K, table, j)
    score = lax.dot_general(query, jnp.concatenate(keys, axis=0), NT, preferred_element_type=F32)
    score = score * COEF
    return jnp.concatenate([score[:, :own], score[:, own:] + bias], axis=1)


def weigh(weight, sources, cols, table, j):
    vals = keys_of(sources, cols, ROWS, ROWS) + pieces_of(sources, cols, HIST_V, table, j)
    vals = jnp.concatenate(vals, axis=0)
    vals = jnp.concatenate([vals, jnp.ones(vals.shape, BF)], axis=1)
    return jnp.dot(weight.astype(BF), vals, preferred_element_type=F32)


def near_kernel(base, count, table, *refs):
    queries, sources = refs[:count], refs[count : count + 2]
    out, stat = refs[count + 2 :]
    lane = lax.broadcasted_iota(jnp.int32, (ROWS, HDIM), 1)
    stat[...] = jnp.zeros(stat.shape, F32)
    bias = biases_of(table, base, count)
    for h in range(HEADS):
        cols = slice(h * HDIM, (h + 1) * HDIM)
        for j in range(count):
            score = scores_of(queries[j][:, cols], sources, cols, table, bias[j], base + j)
            top = jnp.max(score, axis=1, keepdims=True)
            num = weigh(jnp.exp2(score - top), sources, cols, table, base + j)
            total = num[:, HDIM:]
            out[j, :, cols] = num[:, :HDIM] / total
            stat[j] = jnp.where(lane == h, top + jnp.log2(total), stat[j])


def near_pass(base, table, queries, sources):
    count = len(queries)
    return call(
        functools.partial(near_kernel, base, count),
        [
            jax.ShapeDtypeStruct((count, ROWS, WIDTH), F32),
            jax.ShapeDtypeStruct((count, ROWS, HDIM), F32),
        ],
        [SMEM] + [VMEM] * (count + 2),
        (table, *queries, *sources),
        out_specs=[VMEM, VMEM],
    )


def split3(value):
    hi = value.astype(BF).astype(F32)
    mid = (value - hi).astype(BF).astype(F32)
    return [hi, mid, value - hi - mid]


def write_level(out, level):
    tile = jnp.concatenate(split3(level) + [jnp.zeros((EXTRA - 3 * HEADS, 256), F32)], axis=0)
    tile = jnp.concatenate([tile, jnp.zeros((EXTRA, WIDTH - 256), F32)], axis=1)
    out[ROWS : ROWS + EXTRA, :] = tile.astype(BF)


def read_level(ref):
    tile = ref[ROWS : ROWS + EXTRA, 0:256].astype(F32)
    return tile[:HEADS] + tile[HEADS : 2 * HEADS] + tile[2 * HEADS : 3 * HEADS]


def far_kernel(base, offset, count, table, *refs):
    queries, (state, level), sources = refs[:count], refs[count : count + 2], refs[count + 2 : count + 4]
    outs, stat = refs[count + 4 : 2 * count + 4], refs[2 * count + 4]
    lane = lax.broadcasted_iota(jnp.int32, (ROWS, HDIM), 1)
    stat[...] = jnp.zeros(stat.shape, F32)
    bias = biases_of(table, base, count)
    for h in range(HEADS):
        cols = slice(h * HDIM, (h + 1) * HDIM)
        for j in range(count):
            score = scores_of(queries[j][:, cols], sources, cols, table, bias[j], base + j)
            before = jnp.where(lane == h, level[offset + j], 0.0)
            before = jnp.sum(before, axis=1, keepdims=True)
            top = jnp.maximum(jnp.max(score, axis=1, keepdims=True), before)
            num = weigh(jnp.exp2(score - top), sources, cols, table, base + j)
            keep = jnp.exp2(before - top)
            total = num[:, HDIM:] + keep
            num = (num[:, :HDIM] + state[offset + j, :, cols] * keep) / total
            outs[j][0:ROWS, cols] = num.astype(BF)
            stat[j, 0:ROWS, :] = jnp.where(lane == h, top + jnp.log2(total), stat[j, 0:ROWS, :])
    for j in range(count):
        write_level(outs[j], jnp.transpose(stat[j])[0:HEADS, :])


def far_pass(base, offset, table, queries, states, sources):
    count = len(queries)
    return call(
        functools.partial(far_kernel, base + offset, offset, count),
        [jax.ShapeDtypeStruct((ROWS + EXTRA, WIDTH), BF)] * count,
        [SMEM] + [VMEM] * (count + 4),
        (table, *queries, *states, *sources),
        out_specs=[VMEM] * count,
        scratch_shapes=[pltpu.VMEM((count, 256, HDIM), F32)],
    )


def merge_kernel(last, *refs):
    refs, out = refs[:-1], refs[-1]
    levels = [read_level(r) for r in refs]
    top = functools.reduce(jnp.maximum, levels)
    shares = [jnp.exp2(v - top) for v in levels]
    total = functools.reduce(jnp.add, shares)
    rest = jnp.zeros((8 - HEADS, 256), F32)
    stacked = []
    for s in shares:
        stacked += [s / total, rest]
    stacked.append(jnp.zeros((HDIM - 8 * len(refs), 256), F32))
    columns = jnp.transpose(jnp.concatenate(stacked, axis=0))
    for h in range(HEADS):
        cols = slice(h * HDIM, (h + 1) * HDIM)
        acc = None
        for i, ref in enumerate(refs):
            at = 8 * i + h
            part = ref[0:ROWS, cols].astype(F32) * columns[0:ROWS, at : at + 1]
            acc = part if acc is None else acc + part
        out[0:ROWS, cols] = acc.astype(BF)
    if not last:
        write_level(out, top + jnp.log2(total))


def merge(*args, last=False):
    return call(
        functools.partial(merge_kernel, last),
        jax.ShapeDtypeStruct((ROWS if last else ROWS + EXTRA, WIDTH), BF),
        [VMEM] * len(args),
        args,
        mib=6,
        out_specs=VMEM,
    )


def send_home(part):
    own = merge(home(part[0, 4]), part[0, 3])
    other = merge(home(part[1, 3]), part[1, 2])
    own = merge(home(own), part[0, 2])
    other = merge(home(other), part[1, 1])
    own = merge(home(own), part[0, 1])
    other = swap_core(home(other))
    return merge(home(own), other, part[0, 0], last=True)


def project_kernel(count, *refs):
    values, mine, other = refs[:count], refs[count : 2 * count], refs[2 * count : 3 * count]
    before, outs = refs[3 * count : -2], refs[-2:]
    sums = [r[...] for r in before] or [None, None]
    for k, weights in enumerate((mine, other)):
        for v, w in zip(values, weights, strict=True):
            part = jnp.dot(v[...], w[...], preferred_element_type=F32)
            sums[k] = part if sums[k] is None else sums[k] + part
    outs[0][...], outs[1][...] = sums


def project(values, mine, other, before=()):
    count = len(values)
    return call(
        functools.partial(project_kernel, count),
        [jax.ShapeDtypeStruct((ROWS, WIDTH), F32)] * 2,
        [VMEM] * (3 * count + len(before)),
        (*values, *mine, *other, *before),
        out_specs=[VMEM] * 2,
    )


def finish_kernel(choice, flag, value, mine, other, before_mine, before_other, out):
    sides = ((mine, before_mine, choice), (other, before_other, 1 - choice))
    for weights, before, taken in sides:

        @pl.when(flag[0] == taken)
        def _():
            total = before[...] + jnp.dot(value[...], weights[...], preferred_element_type=F32)
            out[...] = total.astype(out.dtype)


def finish(choice, flag, value, mine, other, before, kind, cost):
    return call(
        functools.partial(finish_kernel, choice),
        jax.ShapeDtypeStruct((ROWS, WIDTH), kind),
        [SMEM] + [VMEM] * 5,
        (flag, value, mine, other, *before),
        cost=cost,
        out_specs=VMEM,
    )


def gather_queries(queries):
    asked = {(0, 0): queries, (1, 0): swap_core(queries)}
    for k in range(1, 5):
        for side in range(2 if k < 4 else 1):
            asked[side, k] = away(asked[side, k - 1])
    return asked


def route_kernel(place, first, second, out):
    me = place[0]
    core = me & 1
    lane = lax.broadcasted_iota(jnp.int32, (8, HDIM), 1)
    row = lax.broadcasted_iota(jnp.int32, (8, HDIM), 0)
    piece = lane.astype(F32)
    wanted = jnp.zeros((8, HDIM), jnp.int32)
    for j, (side, k) in enumerate(BLOCKS):
        column = me + side * (1 - 2 * core)
        wanted = jnp.where(row == j, (column + 4 * k * (2 * core - 1)) & 31, wanted)
    wanted = wanted.astype(F32)
    found = jnp.zeros((8, HDIM), F32)
    for g, tail in enumerate((first, second)):
        readers = tail[...].astype(F32)
        hit = (readers[0:1, :] == wanted) | (readers[1:2, :] == wanted)
        hit = hit & (lane < HELD)
        low = jnp.min(jnp.where(hit, piece, HELD), axis=1, keepdims=True)
        high = jnp.max(jnp.where(hit, piece, -1.0), axis=1, keepdims=True)
        found = jnp.where(lane == 2 * g, jnp.minimum(low, HELD - 1.0), found)
        found = jnp.where(lane == 2 * g + 1, jnp.maximum(high, 0.0), found)
        found = jnp.where(lane == 2 * g + 4, jnp.where(high >= 0.0, 1.0, 0.0), found)
        found = jnp.where(lane == 2 * g + 5, jnp.where(high > low, 1.0, 0.0), found)
    out[...] = found.astype(jnp.int32)


def routes(place, first, second):
    return call(
        route_kernel,
        jax.ShapeDtypeStruct((8, HDIM), jnp.int32),
        [SMEM, VMEM, VMEM],
        (place, first[TAIL:, :HDIM], second[TAIL:, :HDIM]),
        mib=4,
        out_specs=VMEM,
    )


def local(queries, cur_keys, cur_values, hist_keys, hist_values, piece_readers, out_weight):
    me = lax.axis_index("seq")
    core = lax.rem(me, 2)
    spot = lax.axis_index("head")
    y, x_hi = lax.rem(spot, YS), spot // YS
    place = me.reshape(1).astype(jnp.int32)

    held = pack(cur_keys, cur_values, hist_keys, hist_values, piece_readers.T)
    held_x = swap_x(held)
    asked = gather_queries(queries)
    held_c = swap_core(held)
    step = 1 - 2 * core
    spread = after(out_weight, held_c)

    def piece(half, r):
        start = (half * YS + lax.rem(y + r + YS, YS)) * WIDTH
        return lax.dynamic_slice_in_dim(spread, start, WIDTH, 1)

    relay = y_move(piece(core, 2), 1)
    table = routes(place, held, held_c)
    lined = [[asked[b] for b in group] for group in GROUPS]
    states = [near_pass(0, table, lined[0], (held, held_c))]
    ready = after(table, states[0][0])
    states.append(near_pass(3, ready, lined[1], (held, held_c)))
    one = y_move(piece(core, step), 1)
    ready = after(table, relay, one, states[1][0])
    states.append(near_pass(5, ready, lined[2], (held, held_c)))
    held_xc = swap_core(after(held_x, states[2][0]))
    three = y_move(after(piece(core, -step), asked[0, 3]), -1)
    two = y_move(after(relay, asked[0, 3]), 1)
    table = routes(place, held_x, held_xc)
    part = {}
    for g, base, offset, count in FAR:
        blocks = GROUPS[g][offset : offset + count]
        outs = far_pass(base, offset, table, [asked[b] for b in blocks], states[g], (held_x, held_xc))
        part.update(zip(blocks, outs, strict=True))
    attended = send_home(part)
    mine = [piece(core, 0), one, three, two]
    other = [piece(1 - core, 0)] + [swap_core(w) for w in (three, one, two)]
    near_y = y_move(attended, 1)
    across = y_move(near_y, 1)
    sums = project([attended], mine[:1], other[:1])
    far_y = y_move(after(attended, sums[0]), -1)
    sums = project([near_y, far_y], mine[1:3], other[1:3], sums)
    flag = (core == x_hi).reshape(1).astype(jnp.int32)
    send = finish(0, flag, across, mine[3], other[3], sums, BF, SMALL)
    keep = finish(1, flag, after(across, send), mine[3], other[3], sums, F32, LONG)
    return (keep + swap_x_hi(send).astype(F32)).astype(BF)


def solution(mesh):
    placed = (
        P("seq", "head"),
        P("seq", "head"),
        P("seq", "head"),
        P("seq", "head"),
        P("seq", "head"),
        P("seq", None),
        P("head", None),
    )
    return jax.shard_map(
        local, mesh=mesh, in_specs=placed, out_specs=P("seq", "head"), check_vma=False
    )
```

```python
import functools
import math

import jax
import jax.numpy as jnp
from jax import lax
from jax.experimental import pallas as pl
from jax.experimental.pallas import tpu as pltpu
from jax.sharding import PartitionSpec as P

HDIM = 128
HEADS = 5
PLANES = 8
ROWS = 192
EXTRA = 16
HIST = 448
TAIL = 2 * (ROWS + HIST)
HELD_ROWS = TAIL + 16
PIECE = 32
HELD = 14
YS = 4
HIST_K = 2 * ROWS
HIST_V = 2 * ROWS + HIST
WIDTH = HEADS * HDIM
COEF = math.log2(math.e) / math.sqrt(HDIM)
NEG = -1e30
GROUPS = (((0, 0), (0, 1), (1, 1)), ((0, 2), (1, 2)), ((0, 3), (1, 3), (0, 4)))
BLOCKS = tuple(b for g in GROUPS for b in g)
FAR = ((2, 5, 2, 1), (2, 5, 0, 2), (1, 3, 0, 2), (0, 0, 0, 3))
BF = jnp.bfloat16
F32 = jnp.float32
NT = (((1,), (1,)), ((), ()))
VMEM = pl.BlockSpec(memory_space=pltpu.VMEM)
SMEM = pl.BlockSpec(memory_space=pltpu.SMEM)
MIB = 1024 * 1024
SMALL = pl.CostEstimate(flops=1000, bytes_accessed=1000, transcendentals=0)
LONG = pl.CostEstimate(flops=5000000000, bytes_accessed=1000, transcendentals=0)
ANY = pl.BlockSpec(memory_space=pl.ANY)


def seq_move(value, to):
    perm = []
    for z in range(PLANES):
        for x in range(2):
            for c in range(2):
                nz, nx, nc = to(z, x, c)
                perm.append((z * 4 + x * 2 + c, (nz % PLANES) * 4 + nx * 2 + nc))
    return lax.ppermute(value, "seq", perm)


def swap_core(value):
    return seq_move(value, lambda z, x, c: (z, x, 1 - c))


def swap_x(value):
    return seq_move(value, lambda z, x, c: (z, 1 - x, c))


def away(value):
    return seq_move(value, lambda z, x, c: (z + 1 - 2 * c, x, c))


def home(value):
    return seq_move(value, lambda z, x, c: (z - 1 + 2 * c, x, c))


def swap_x_hi(value):
    return lax.ppermute(value, "head", [(i, (i + YS) % (2 * YS)) for i in range(2 * YS)])


def y_move(value, sign):
    perm = []
    for s in range(PLANES * 4):
        for x in range(2):
            for y in range(YS):
                to = (y + sign * (1 - 2 * (s % 2))) % YS
                perm.append(((s * 2 + x) * YS + y, (s * 2 + x) * YS + to))
    return lax.ppermute(value, ("seq", "head"), perm)


def after(value, *others):
    return lax.optimization_barrier((value, *others))[0]


def call(kernel, shapes, specs, args, mib=8, cost=SMALL, **more):
    return pl.pallas_call(
        kernel,
        out_shape=shapes,
        in_specs=specs,
        compiler_params=pltpu.CompilerParams(vmem_limit_bytes=mib * MIB),
        cost_estimate=cost,
        **more,
    )(*args)


def pack_kernel(cur_k, cur_v, hist_k, hist_v, readers, out, room, came, gone):
    rows = ((hist_k, HIST_K, HIST), (hist_v, HIST_V, HIST), (cur_k, 0, ROWS), (cur_v, ROWS, ROWS))
    reads, writes = [], []
    for i, (ref, at, size) in enumerate(rows):
        part = room.at[pl.ds(at, size), :]
        reads.append(pltpu.make_async_copy(ref, part, came.at[i]))
        writes.append(pltpu.make_async_copy(part, out.at[pl.ds(at, size), :], gone.at[i]))
    for read in reads:
        read.start()
    named = readers[...].astype(F32)
    named = jnp.concatenate([named, jnp.zeros((2, WIDTH - HELD), F32)], axis=1)
    named = jnp.concatenate([named, jnp.zeros((14, WIDTH), F32)], axis=0)
    room[TAIL:HELD_ROWS, :] = named.astype(BF)
    last = pltpu.make_async_copy(
        room.at[pl.ds(TAIL, 16), :], out.at[pl.ds(TAIL, 16), :], gone.at[4]
    )
    last.start()
    for read, write in zip(reads, writes, strict=True):
        read.wait()
        write.start()
    for write in writes:
        write.wait()
    last.wait()


def pack(*raw):
    return call(
        pack_kernel,
        jax.ShapeDtypeStruct((HELD_ROWS, WIDTH), BF),
        [ANY] * 4 + [VMEM],
        raw,
        mib=60,
        out_specs=ANY,
        scratch_shapes=[
            pltpu.VMEM((HELD_ROWS, WIDTH), BF),
            pltpu.SemaphoreType.DMA((4,)),
            pltpu.SemaphoreType.DMA((5,)),
        ],
    )


def keys_of(sources, cols, start, count):
    return [s[start : start + count, cols] for s in sources]


def pieces_of(sources, cols, start, table, j):
    found = []
    for t in range(4):
        at = pl.multiple_of(start + table[j, t] * PIECE, PIECE)
        found.append(sources[t // 2][pl.ds(at, PIECE), cols])
    return found


def biases_of(table, base, count):
    slot = lax.broadcasted_iota(jnp.int32, (1, 4 * PIECE), 1) >> 5
    rows = []
    for j in range(base, base + count):
        row = jnp.zeros((1, 4 * PIECE), F32)
        for t in range(4):
            row = jnp.where(slot == t, (1 - table[j, 4 + t]).astype(F32) * NEG, row)
        rows.append(row)
    return rows


def scores_of(query, sources, cols, table, bias, j):
    own = 2 * ROWS
    keys = keys_of(sources, cols, 0, ROWS) + pieces_of(sources, cols, HIST_K, table, j)
    score = lax.dot_general(query, jnp.concatenate(keys, axis=0), NT, preferred_element_type=F32)
    score = score * COEF
    return jnp.concatenate([score[:, :own], score[:, own:] + bias], axis=1)


def weigh(weight, sources, cols, table, j):
    vals = keys_of(sources, cols, ROWS, ROWS) + pieces_of(sources, cols, HIST_V, table, j)
    vals = jnp.concatenate(vals, axis=0)
    vals = jnp.concatenate([vals, jnp.ones(vals.shape, BF)], axis=1)
    return jnp.dot(weight.astype(BF), vals, preferred_element_type=F32)


def near_kernel(base, count, table, *refs):
    queries, sources = refs[:count], refs[count : count + 2]
    out, stat = refs[count + 2 :]
    lane = lax.broadcasted_iota(jnp.int32, (ROWS, HDIM), 1)
    stat[...] = jnp.zeros(stat.shape, F32)
    bias = biases_of(table, base, count)
    for h in range(HEADS):
        cols = slice(h * HDIM, (h + 1) * HDIM)
        for j in range(count):
            score = scores_of(queries[j][:, cols], sources, cols, table, bias[j], base + j)
            top = jnp.max(score, axis=1, keepdims=True)
            num = weigh(jnp.exp2(score - top), sources, cols, table, base + j)
            total = num[:, HDIM:]
            out[j, :, cols] = num[:, :HDIM] / total
            stat[j] = jnp.where(lane == h, top + jnp.log2(total), stat[j])


def near_pass(base, table, queries, sources):
    count = len(queries)
    return call(
        functools.partial(near_kernel, base, count),
        [
            jax.ShapeDtypeStruct((count, ROWS, WIDTH), F32),
            jax.ShapeDtypeStruct((count, ROWS, HDIM), F32),
        ],
        [SMEM] + [VMEM] * (count + 2),
        (table, *queries, *sources),
        out_specs=[VMEM, VMEM],
    )


def split3(value):
    hi = value.astype(BF).astype(F32)
    mid = (value - hi).astype(BF).astype(F32)
    return [hi, mid, value - hi - mid]


def write_level(out, level):
    tile = jnp.concatenate(split3(level) + [jnp.zeros((EXTRA - 3 * HEADS, 256), F32)], axis=0)
    tile = jnp.concatenate([tile, jnp.zeros((EXTRA, WIDTH - 256), F32)], axis=1)
    out[ROWS : ROWS + EXTRA, :] = tile.astype(BF)


def read_level(ref):
    tile = ref[ROWS : ROWS + EXTRA, 0:256].astype(F32)
    return tile[:HEADS] + tile[HEADS : 2 * HEADS] + tile[2 * HEADS : 3 * HEADS]


def far_kernel(base, offset, count, table, *refs):
    queries, (state, level), sources = refs[:count], refs[count : count + 2], refs[count + 2 : count + 4]
    outs, stat = refs[count + 4 : 2 * count + 4], refs[2 * count + 4]
    lane = lax.broadcasted_iota(jnp.int32, (ROWS, HDIM), 1)
    stat[...] = jnp.zeros(stat.shape, F32)
    bias = biases_of(table, base, count)
    for h in range(HEADS):
        cols = slice(h * HDIM, (h + 1) * HDIM)
        for j in range(count):
            score = scores_of(queries[j][:, cols], sources, cols, table, bias[j], base + j)
            before = jnp.where(lane == h, level[offset + j], 0.0)
            before = jnp.sum(before, axis=1, keepdims=True)
            top = jnp.maximum(jnp.max(score, axis=1, keepdims=True), before)
            num = weigh(jnp.exp2(score - top), sources, cols, table, base + j)
            keep = jnp.exp2(before - top)
            total = num[:, HDIM:] + keep
            num = (num[:, :HDIM] + state[offset + j, :, cols] * keep) / total
            outs[j][0:ROWS, cols] = num.astype(BF)
            stat[j, 0:ROWS, :] = jnp.where(lane == h, top + jnp.log2(total), stat[j, 0:ROWS, :])
    for j in range(count):
        write_level(outs[j], jnp.transpose(stat[j])[0:HEADS, :])


def far_pass(base, offset, table, queries, states, sources):
    count = len(queries)
    return call(
        functools.partial(far_kernel, base + offset, offset, count),
        [jax.ShapeDtypeStruct((ROWS + EXTRA, WIDTH), BF)] * count,
        [SMEM] + [VMEM] * (count + 4),
        (table, *queries, *states, *sources),
        out_specs=[VMEM] * count,
        scratch_shapes=[pltpu.VMEM((count, 256, HDIM), F32)],
    )


def merge_kernel(last, *refs):
    refs, out = refs[:-1], refs[-1]
    levels = [read_level(r) for r in refs]
    top = functools.reduce(jnp.maximum, levels)
    shares = [jnp.exp2(v - top) for v in levels]
    total = functools.reduce(jnp.add, shares)
    rest = jnp.zeros((8 - HEADS, 256), F32)
    stacked = []
    for s in shares:
        stacked += [s / total, rest]
    stacked.append(jnp.zeros((HDIM - 8 * len(refs), 256), F32))
    columns = jnp.transpose(jnp.concatenate(stacked, axis=0))
    for h in range(HEADS):
        cols = slice(h * HDIM, (h + 1) * HDIM)
        acc = None
        for i, ref in enumerate(refs):
            at = 8 * i + h
            part = ref[0:ROWS, cols].astype(F32) * columns[0:ROWS, at : at + 1]
            acc = part if acc is None else acc + part
        out[0:ROWS, cols] = acc.astype(BF)
    if not last:
        write_level(out, top + jnp.log2(total))


def merge(*args, last=False):
    return call(
        functools.partial(merge_kernel, last),
        jax.ShapeDtypeStruct((ROWS if last else ROWS + EXTRA, WIDTH), BF),
        [VMEM] * len(args),
        args,
        mib=6,
        out_specs=VMEM,
    )


def send_home(part):
    own = merge(home(part[0, 4]), part[0, 3])
    other = merge(home(part[1, 3]), part[1, 2])
    own = merge(home(own), part[0, 2])
    other = merge(home(other), part[1, 1])
    own = merge(home(own), part[0, 1])
    other = swap_core(home(other))
    return merge(home(own), other, part[0, 0], last=True)


def project_kernel(count, *refs):
    values, mine, other = refs[:count], refs[count : 2 * count], refs[2 * count : 3 * count]
    before, outs = refs[3 * count : -2], refs[-2:]
    sums = [r[...] for r in before] or [None, None]
    for k, weights in enumerate((mine, other)):
        for v, w in zip(values, weights, strict=True):
            part = jnp.dot(v[...], w[...], preferred_element_type=F32)
            sums[k] = part if sums[k] is None else sums[k] + part
    outs[0][...], outs[1][...] = sums


def project(values, mine, other, before=()):
    count = len(values)
    return call(
        functools.partial(project_kernel, count),
        [jax.ShapeDtypeStruct((ROWS, WIDTH), F32)] * 2,
        [VMEM] * (3 * count + len(before)),
        (*values, *mine, *other, *before),
        out_specs=[VMEM] * 2,
    )


def finish_kernel(choice, flag, value, mine, other, before_mine, before_other, out):
    sides = ((mine, before_mine, choice), (other, before_other, 1 - choice))
    for weights, before, taken in sides:

        @pl.when(flag[0] == taken)
        def _():
            total = before[...] + jnp.dot(value[...], weights[...], preferred_element_type=F32)
            out[...] = total.astype(out.dtype)


def finish(choice, flag, value, mine, other, before, kind, cost):
    return call(
        functools.partial(finish_kernel, choice),
        jax.ShapeDtypeStruct((ROWS, WIDTH), kind),
        [SMEM] + [VMEM] * 5,
        (flag, value, mine, other, *before),
        cost=cost,
        out_specs=VMEM,
    )


def gather_queries(queries):
    asked = {(0, 0): queries, (1, 0): swap_core(queries)}
    for k in range(1, 5):
        for side in range(2 if k < 4 else 1):
            asked[side, k] = away(asked[side, k - 1])
    return asked


def route_kernel(place, first, second, out):
    me = place[0]
    core = me & 1
    lane = lax.broadcasted_iota(jnp.int32, (8, HDIM), 1)
    row = lax.broadcasted_iota(jnp.int32, (8, HDIM), 0)
    piece = lane.astype(F32)
    wanted = jnp.zeros((8, HDIM), jnp.int32)
    for j, (side, k) in enumerate(BLOCKS):
        column = me + side * (1 - 2 * core)
        wanted = jnp.where(row == j, (column + 4 * k * (2 * core - 1)) & 31, wanted)
    wanted = wanted.astype(F32)
    found = jnp.zeros((8, HDIM), F32)
    for g, tail in enumerate((first, second)):
        readers = tail[...].astype(F32)
        hit = (readers[0:1, :] == wanted) | (readers[1:2, :] == wanted)
        hit = hit & (lane < HELD)
        low = jnp.min(jnp.where(hit, piece, HELD), axis=1, keepdims=True)
        high = jnp.max(jnp.where(hit, piece, -1.0), axis=1, keepdims=True)
        found = jnp.where(lane == 2 * g, jnp.minimum(low, HELD - 1.0), found)
        found = jnp.where(lane == 2 * g + 1, jnp.maximum(high, 0.0), found)
        found = jnp.where(lane == 2 * g + 4, jnp.where(high >= 0.0, 1.0, 0.0), found)
        found = jnp.where(lane == 2 * g + 5, jnp.where(high > low, 1.0, 0.0), found)
    out[...] = found.astype(jnp.int32)


def routes(place, first, second):
    return call(
        route_kernel,
        jax.ShapeDtypeStruct((8, HDIM), jnp.int32),
        [SMEM, VMEM, VMEM],
        (place, first[TAIL:, :HDIM], second[TAIL:, :HDIM]),
        mib=4,
        out_specs=VMEM,
    )


def local(queries, cur_keys, cur_values, hist_keys, hist_values, piece_readers, out_weight):
    me = lax.axis_index("seq")
    core = lax.rem(me, 2)
    spot = lax.axis_index("head")
    y, x_hi = lax.rem(spot, YS), spot // YS
    place = me.reshape(1).astype(jnp.int32)

    held = pack(cur_keys, cur_values, hist_keys, hist_values, piece_readers.T)
    held_x = swap_x(held)
    asked = gather_queries(queries)
    held_c = swap_core(held)
    step = 1 - 2 * core
    spread = after(out_weight, held_c)

    def piece(half, r):
        start = (half * YS + lax.rem(y + r + YS, YS)) * WIDTH
        return lax.dynamic_slice_in_dim(spread, start, WIDTH, 1)

    relay = y_move(piece(core, 2), 1)
    table = routes(place, held, held_c)
    lined = [[asked[b] for b in group] for group in GROUPS]
    states = [near_pass(0, table, lined[0], (held, held_c))]
    ready = after(table, states[0][0])
    states.append(near_pass(3, ready, lined[1], (held, held_c)))
    one = y_move(piece(core, step), 1)
    ready = after(table, relay, one, states[1][0])
    states.append(near_pass(5, ready, lined[2], (held, held_c)))
    held_xc = swap_core(after(held_x, states[2][0]))
    three = y_move(after(piece(core, -step), asked[0, 2]), -1)
    two = y_move(after(relay, asked[0, 3]), 1)
    table = routes(place, held_x, held_xc)
    part = {}
    for g, base, offset, count in FAR:
        blocks = GROUPS[g][offset : offset + count]
        outs = far_pass(base, offset, table, [asked[b] for b in blocks], states[g], (held_x, held_xc))
        part.update(zip(blocks, outs, strict=True))
    attended = send_home(part)
    mine = [piece(core, 0), one, three, two]
    other = [piece(1 - core, 0)] + [swap_core(w) for w in (three, one, two)]
    near_y = y_move(attended, 1)
    across = y_move(near_y, 1)
    sums = project([attended], mine[:1], other[:1])
    far_y = y_move(after(attended, sums[0]), -1)
    sums = project([near_y, far_y], mine[1:3], other[1:3], sums)
    flag = (core == x_hi).reshape(1).astype(jnp.int32)
    send = finish(0, flag, across, mine[3], other[3], sums, BF, SMALL)
    keep = finish(1, flag, after(across, send), mine[3], other[3], sums, F32, LONG)
    return (keep + swap_x_hi(send).astype(F32)).astype(BF)


def solution(mesh):
    placed = (
        P("seq", "head"),
        P("seq", "head"),
        P("seq", "head"),
        P("seq", "head"),
        P("seq", "head"),
        P("seq", None),
        P("head", None),
    )
    return jax.shard_map(
        local, mesh=mesh, in_specs=placed, out_specs=P("seq", "head"), check_vma=False
    )
```

```python
import functools
import math

import jax
import jax.numpy as jnp
from jax import lax
from jax.experimental import pallas as pl
from jax.experimental.pallas import tpu as pltpu
from jax.sharding import PartitionSpec as P

HDIM = 128
HEADS = 5
PLANES = 8
ROWS = 192
EXTRA = 16
HIST = 448
TAIL = 2 * (ROWS + HIST)
HELD_ROWS = TAIL + 16
PIECE = 32
HELD = 14
YS = 4
HIST_K = 2 * ROWS
HIST_V = 2 * ROWS + HIST
WIDTH = HEADS * HDIM
COEF = math.log2(math.e) / math.sqrt(HDIM)
NEG = -1e30
GROUPS = (((0, 0), (0, 1), (1, 1)), ((0, 2), (1, 2)), ((0, 3), (1, 3), (0, 4)))
BLOCKS = tuple(b for g in GROUPS for b in g)
FAR = ((2, 5, 2, 1), (2, 5, 0, 2), (1, 3, 0, 2), (0, 0, 0, 3))
BF = jnp.bfloat16
F32 = jnp.float32
NT = (((1,), (1,)), ((), ()))
VMEM = pl.BlockSpec(memory_space=pltpu.VMEM)
SMEM = pl.BlockSpec(memory_space=pltpu.SMEM)
MIB = 1024 * 1024
SMALL = pl.CostEstimate(flops=1000, bytes_accessed=1000, transcendentals=0)
LONG = pl.CostEstimate(flops=5000000000, bytes_accessed=1000, transcendentals=0)
ANY = pl.BlockSpec(memory_space=pl.ANY)


def seq_move(value, to):
    perm = []
    for z in range(PLANES):
        for x in range(2):
            for c in range(2):
                nz, nx, nc = to(z, x, c)
                perm.append((z * 4 + x * 2 + c, (nz % PLANES) * 4 + nx * 2 + nc))
    return lax.ppermute(value, "seq", perm)


def swap_core(value):
    return seq_move(value, lambda z, x, c: (z, x, 1 - c))


def swap_x(value):
    return seq_move(value, lambda z, x, c: (z, 1 - x, c))


def away(value):
    return seq_move(value, lambda z, x, c: (z + 1 - 2 * c, x, c))


def home(value):
    return seq_move(value, lambda z, x, c: (z - 1 + 2 * c, x, c))


def swap_x_hi(value):
    return lax.ppermute(value, "head", [(i, (i + YS) % (2 * YS)) for i in range(2 * YS)])


def y_move(value, sign):
    perm = []
    for s in range(PLANES * 4):
        for x in range(2):
            for y in range(YS):
                to = (y + sign * (1 - 2 * (s % 2))) % YS
                perm.append(((s * 2 + x) * YS + y, (s * 2 + x) * YS + to))
    return lax.ppermute(value, ("seq", "head"), perm)


def after(value, *others):
    return lax.optimization_barrier((value, *others))[0]


def call(kernel, shapes, specs, args, mib=12, cost=SMALL, **more):
    return pl.pallas_call(
        kernel,
        out_shape=shapes,
        in_specs=specs,
        compiler_params=pltpu.CompilerParams(vmem_limit_bytes=mib * MIB),
        cost_estimate=cost,
        **more,
    )(*args)


def pack_kernel(cur_k, cur_v, hist_k, hist_v, readers, out, room, came, gone):
    rows = ((hist_k, HIST_K, HIST), (hist_v, HIST_V, HIST), (cur_k, 0, ROWS), (cur_v, ROWS, ROWS))
    reads, writes = [], []
    for i, (ref, at, size) in enumerate(rows):
        part = room.at[pl.ds(at, size), :]
        reads.append(pltpu.make_async_copy(ref, part, came.at[i]))
        writes.append(pltpu.make_async_copy(part, out.at[pl.ds(at, size), :], gone.at[i]))
    for read in reads:
        read.start()
    named = readers[...].astype(F32)
    named = jnp.concatenate([named, jnp.zeros((2, WIDTH - HELD), F32)], axis=1)
    named = jnp.concatenate([named, jnp.zeros((14, WIDTH), F32)], axis=0)
    room[TAIL:HELD_ROWS, :] = named.astype(BF)
    last = pltpu.make_async_copy(
        room.at[pl.ds(TAIL, 16), :], out.at[pl.ds(TAIL, 16), :], gone.at[4]
    )
    last.start()
    for read, write in zip(reads, writes, strict=True):
        read.wait()
        write.start()
    for write in writes:
        write.wait()
    last.wait()


def pack(*raw):
    return call(
        pack_kernel,
        jax.ShapeDtypeStruct((HELD_ROWS, WIDTH), BF),
        [ANY] * 4 + [VMEM],
        raw,
        mib=60,
        out_specs=ANY,
        scratch_shapes=[
            pltpu.VMEM((HELD_ROWS, WIDTH), BF),
            pltpu.SemaphoreType.DMA((4,)),
            pltpu.SemaphoreType.DMA((5,)),
        ],
    )


def keys_of(sources, cols, start, count):
    return [s[start : start + count, cols] for s in sources]


def pieces_of(sources, cols, start, table, j):
    found = []
    for t in range(4):
        at = pl.multiple_of(start + table[j, t] * PIECE, PIECE)
        found.append(sources[t // 2][pl.ds(at, PIECE), cols])
    return found


def biases_of(table, base, count):
    slot = lax.broadcasted_iota(jnp.int32, (1, 4 * PIECE), 1) >> 5
    rows = []
    for j in range(base, base + count):
        row = jnp.zeros((1, 4 * PIECE), F32)
        for t in range(4):
            row = jnp.where(slot == t, (1 - table[j, 4 + t]).astype(F32) * NEG, row)
        rows.append(row)
    return rows


def scores_of(query, sources, cols, table, bias, j):
    own = 2 * ROWS
    keys = keys_of(sources, cols, 0, ROWS) + pieces_of(sources, cols, HIST_K, table, j)
    score = lax.dot_general(query, jnp.concatenate(keys, axis=0), NT, preferred_element_type=F32)
    score = score * COEF
    return jnp.concatenate([score[:, :own], score[:, own:] + bias], axis=1)


def weigh(weight, sources, cols, table, j):
    vals = keys_of(sources, cols, ROWS, ROWS) + pieces_of(sources, cols, HIST_V, table, j)
    vals = jnp.concatenate(vals, axis=0)
    vals = jnp.concatenate([vals, jnp.ones(vals.shape, BF)], axis=1)
    return jnp.dot(weight.astype(BF), vals, preferred_element_type=F32)


def near_kernel(base, count, table, *refs):
    queries, sources = refs[:count], refs[count : count + 2]
    out, stat = refs[count + 2 :]
    bias = biases_of(table, base, count)
    for h in range(HEADS):
        cols = slice(h * HDIM, (h + 1) * HDIM)
        for j in range(count):
            score = scores_of(queries[j][:, cols], sources, cols, table, bias[j], base + j)
            top = jnp.max(score, axis=1, keepdims=True)
            num = weigh(jnp.exp2(score - top), sources, cols, table, base + j)
            total = num[:, HDIM:]
            out[j, :, cols] = num[:, :HDIM] / total
            stat[j, :, cols] = top + jnp.log2(total)


def near_pass(base, table, queries, sources):
    count = len(queries)
    return call(
        functools.partial(near_kernel, base, count),
        [
            jax.ShapeDtypeStruct((count, ROWS, WIDTH), F32),
            jax.ShapeDtypeStruct((count, ROWS, WIDTH), F32),
        ],
        [SMEM] + [VMEM] * (count + 2),
        (table, *queries, *sources),
        out_specs=[VMEM, VMEM],
    )


def split3(value):
    hi = value.astype(BF).astype(F32)
    mid = (value - hi).astype(BF).astype(F32)
    return [hi, mid, value - hi - mid]


def write_level(out, level):
    tile = jnp.concatenate(split3(level) + [jnp.zeros((EXTRA - 3 * HEADS, 256), F32)], axis=0)
    tile = jnp.concatenate([tile, jnp.zeros((EXTRA, WIDTH - 256), F32)], axis=1)
    out[ROWS : ROWS + EXTRA, :] = tile.astype(BF)


def read_level(ref):
    tile = ref[ROWS : ROWS + EXTRA, 0:256].astype(F32)
    return tile[:HEADS] + tile[HEADS : 2 * HEADS] + tile[2 * HEADS : 3 * HEADS]


def far_kernel(base, offset, count, table, *refs):
    queries, (state, level), sources = refs[:count], refs[count : count + 2], refs[count + 2 : count + 4]
    outs, stat = refs[count + 4 : 2 * count + 4], refs[2 * count + 4]
    lane = lax.broadcasted_iota(jnp.int32, (ROWS, HDIM), 1)
    stat[...] = jnp.zeros(stat.shape, F32)
    bias = biases_of(table, base, count)
    for h in range(HEADS):
        cols = slice(h * HDIM, (h + 1) * HDIM)
        for j in range(count):
            score = scores_of(queries[j][:, cols], sources, cols, table, bias[j], base + j)
            before = level[offset + j, :, cols]
            top = jnp.maximum(jnp.max(score, axis=1, keepdims=True), before)
            num = weigh(jnp.exp2(score - jnp.concatenate([top] * 4, axis=1)), sources, cols, table, base + j)
            keep = jnp.exp2(before - top)
            total = num[:, HDIM:] + keep
            num = (num[:, :HDIM] + state[offset + j, :, cols] * keep) / total
            outs[j][0:ROWS, cols] = num.astype(BF)
            stat[j, 0:ROWS, :] = jnp.where(lane == h, top + jnp.log2(total), stat[j, 0:ROWS, :])
    for j in range(count):
        write_level(outs[j], jnp.transpose(stat[j])[0:HEADS, :])


def far_pass(base, offset, table, queries, states, sources):
    count = len(queries)
    return call(
        functools.partial(far_kernel, base + offset, offset, count),
        [jax.ShapeDtypeStruct((ROWS + EXTRA, WIDTH), BF)] * count,
        [SMEM] + [VMEM] * (count + 4),
        (table, *queries, *states, *sources),
        out_specs=[VMEM] * count,
        scratch_shapes=[pltpu.VMEM((count, 256, HDIM), F32)],
    )


def merge_kernel(last, *refs):
    refs, out = refs[:-1], refs[-1]
    levels = [read_level(r) for r in refs]
    top = functools.reduce(jnp.maximum, levels)
    shares = [jnp.exp2(v - top) for v in levels]
    total = functools.reduce(jnp.add, shares)
    rest = jnp.zeros((8 - HEADS, 256), F32)
    stacked = []
    for s in shares:
        stacked += [s / total, rest]
    stacked.append(jnp.zeros((HDIM - 8 * len(refs), 256), F32))
    columns = jnp.transpose(jnp.concatenate(stacked, axis=0))
    for h in range(HEADS):
        cols = slice(h * HDIM, (h + 1) * HDIM)
        acc = None
        for i, ref in enumerate(refs):
            at = 8 * i + h
            part = ref[0:ROWS, cols].astype(F32) * columns[0:ROWS, at : at + 1]
            acc = part if acc is None else acc + part
        out[0:ROWS, cols] = acc.astype(BF)
    if not last:
        write_level(out, top + jnp.log2(total))


def merge(*args, last=False):
    return call(
        functools.partial(merge_kernel, last),
        jax.ShapeDtypeStruct((ROWS if last else ROWS + EXTRA, WIDTH), BF),
        [VMEM] * len(args),
        args,
        mib=6,
        out_specs=VMEM,
    )


def send_home(part):
    own = merge(home(part[0, 4]), part[0, 3])
    other = merge(home(part[1, 3]), part[1, 2])
    own = merge(home(own), part[0, 2])
    other = merge(home(other), part[1, 1])
    own = merge(home(own), part[0, 1])
    other = swap_core(home(other))
    return merge(home(own), other, part[0, 0], last=True)


def project_kernel(count, *refs):
    values, mine, other = refs[:count], refs[count : 2 * count], refs[2 * count : 3 * count]
    before, outs = refs[3 * count : -2], refs[-2:]
    sums = [r[...] for r in before] or [None, None]
    for k, weights in enumerate((mine, other)):
        for v, w in zip(values, weights, strict=True):
            part = jnp.dot(v[...], w[...], preferred_element_type=F32)
            sums[k] = part if sums[k] is None else sums[k] + part
    outs[0][...], outs[1][...] = sums


def project(values, mine, other, before=()):
    count = len(values)
    return call(
        functools.partial(project_kernel, count),
        [jax.ShapeDtypeStruct((ROWS, WIDTH), F32)] * 2,
        [VMEM] * (3 * count + len(before)),
        (*values, *mine, *other, *before),
        out_specs=[VMEM] * 2,
    )


def finish_kernel(choice, flag, value, mine, other, before_mine, before_other, out):
    sides = ((mine, before_mine, choice), (other, before_other, 1 - choice))
    for weights, before, taken in sides:

        @pl.when(flag[0] == taken)
        def _():
            total = before[...] + jnp.dot(value[...], weights[...], preferred_element_type=F32)
            out[...] = total.astype(out.dtype)


def finish(choice, flag, value, mine, other, before, kind, cost):
    return call(
        functools.partial(finish_kernel, choice),
        jax.ShapeDtypeStruct((ROWS, WIDTH), kind),
        [SMEM] + [VMEM] * 5,
        (flag, value, mine, other, *before),
        cost=cost,
        out_specs=VMEM,
    )


def gather_queries(queries):
    asked = {(0, 0): queries, (1, 0): swap_core(queries)}
    for k in range(1, 5):
        for side in range(2 if k < 4 else 1):
            asked[side, k] = away(asked[side, k - 1])
    return asked


def route_kernel(place, first, second, out):
    me = place[0]
    core = me & 1
    lane = lax.broadcasted_iota(jnp.int32, (8, HDIM), 1)
    row = lax.broadcasted_iota(jnp.int32, (8, HDIM), 0)
    piece = lane.astype(F32)
    wanted = jnp.zeros((8, HDIM), jnp.int32)
    for j, (side, k) in enumerate(BLOCKS):
        column = me + side * (1 - 2 * core)
        wanted = jnp.where(row == j, (column + 4 * k * (2 * core - 1)) & 31, wanted)
    wanted = wanted.astype(F32)
    found = jnp.zeros((8, HDIM), F32)
    for g, tail in enumerate((first, second)):
        readers = tail[...].astype(F32)
        hit = (readers[0:1, :] == wanted) | (readers[1:2, :] == wanted)
        hit = hit & (lane < HELD)
        low = jnp.min(jnp.where(hit, piece, HELD), axis=1, keepdims=True)
        high = jnp.max(jnp.where(hit, piece, -1.0), axis=1, keepdims=True)
        found = jnp.where(lane == 2 * g, jnp.minimum(low, HELD - 1.0), found)
        found = jnp.where(lane == 2 * g + 1, jnp.maximum(high, 0.0), found)
        found = jnp.where(lane == 2 * g + 4, jnp.where(high >= 0.0, 1.0, 0.0), found)
        found = jnp.where(lane == 2 * g + 5, jnp.where(high > low, 1.0, 0.0), found)
    out[...] = found.astype(jnp.int32)


def routes(place, first, second):
    return call(
        route_kernel,
        jax.ShapeDtypeStruct((8, HDIM), jnp.int32),
        [SMEM, VMEM, VMEM],
        (place, first[TAIL:, :HDIM], second[TAIL:, :HDIM]),
        mib=4,
        out_specs=VMEM,
    )


def local(queries, cur_keys, cur_values, hist_keys, hist_values, piece_readers, out_weight):
    me = lax.axis_index("seq")
    core = lax.rem(me, 2)
    spot = lax.axis_index("head")
    y, x_hi = lax.rem(spot, YS), spot // YS
    place = me.reshape(1).astype(jnp.int32)

    held = pack(cur_keys, cur_values, hist_keys, hist_values, piece_readers.T)
    held_x = swap_x(held)
    asked = gather_queries(queries)
    held_c = swap_core(held)
    step = 1 - 2 * core
    spread = after(out_weight, held_c)

    def piece(half, r):
        start = (half * YS + lax.rem(y + r + YS, YS)) * WIDTH
        return lax.dynamic_slice_in_dim(spread, start, WIDTH, 1)

    relay = y_move(piece(core, 2), 1)
    table = routes(place, held, held_c)
    lined = [[asked[b] for b in group] for group in GROUPS]
    states = [near_pass(0, table, lined[0], (held, held_c))]
    ready = after(table, states[0][0])
    states.append(near_pass(3, ready, lined[1], (held, held_c)))
    one = y_move(piece(core, step), 1)
    ready = after(table, relay, one, states[1][0])
    states.append(near_pass(5, ready, lined[2], (held, held_c)))
    held_xc = swap_core(after(held_x, states[2][0]))
    three = y_move(after(piece(core, -step), asked[0, 3]), -1)
    two = y_move(after(relay, asked[0, 3]), 1)
    table = routes(place, held_x, held_xc)
    part = {}
    for g, base, offset, count in FAR:
        blocks = GROUPS[g][offset : offset + count]
        outs = far_pass(base, offset, table, [asked[b] for b in blocks], states[g], (held_x, held_xc))
        part.update(zip(blocks, outs, strict=True))
    attended = send_home(part)
    mine = [piece(core, 0), one, three, two]
    other = [piece(1 - core, 0)] + [swap_core(w) for w in (three, one, two)]
    near_y = y_move(attended, 1)
    across = y_move(near_y, 1)
    sums = project([attended], mine[:1], other[:1])
    far_y = y_move(after(attended, sums[0]), -1)
    sums = project([near_y, far_y], mine[1:3], other[1:3], sums)
    flag = (core == x_hi).reshape(1).astype(jnp.int32)
    send = finish(0, flag, across, mine[3], other[3], sums, BF, SMALL)
    keep = finish(1, flag, after(across, send), mine[3], other[3], sums, F32, LONG)
    return (keep + swap_x_hi(send).astype(F32)).astype(BF)


def solution(mesh):
    placed = (
        P("seq", "head"),
        P("seq", "head"),
        P("seq", "head"),
        P("seq", "head"),
        P("seq", "head"),
        P("seq", None),
        P("head", None),
    )
    return jax.shard_map(
        local, mesh=mesh, in_specs=placed, out_specs=P("seq", "head"), check_vma=False
    )
```
